256 devices in a mesh: dp: 16 (over z, y_hi), head: 16 (over x, y_lo, core).
Axes of the slice: x: 4, y: 4 (y_hi: 2, y_lo: 2; y = y_hi * 2 + y_lo), z: 8, core: 2. Of those that a mesh axis runs over, the one named last changes fastest.
Arguments:
- q_latent: bfloat16 [4096, 1536], P('dp'), may hold values from -6 to 6
- kv_latent: bfloat16 [4096, 576], P('dp'), may hold values from -6 to 6
- q_up: bfloat16 [1536, 24576], P('dp', 'head'), may hold values from -0.15625 to 0.15625
- kv_up: bfloat16 [512, 32768], P('dp', 'head'), may hold values from -0.25 to 0.25
- out_grad: bfloat16 [4096, 16384], P('dp', 'head'), may hold values from -6 to 6
Outputs:
- d_q_latent: bfloat16 [4096, 1536], P('dp', 'head')
- d_kv_latent: bfloat16 [4096, 576], P('dp', 'head')
- grad_blocks: float32 [256, 512, 512], P(('head', 'dp'))
- left_gram: float32 [256, 512, 512], P(('head', 'dp'))
- right_gram: float32 [256, 512, 512], P(('head', 'dp'))
The draws below stay inside these ranges and needn't reach their ends.
All inputs are finite; a program needn't handle non-finite values.
Results may differ from the reference program's by a relative error of at most 0.024.
Values may be sent and summed in bfloat16 or wider, within the bound.
No kernel may reach another device: no remote copies, remote signals or barrier semaphores. Data moves between devices by JAX's collectives and lax.ppermute only.
A program may use at most 128 MiB of HBM per device.

```python
import math
import jax
import jax.numpy as jnp
from jax import lax

HEADS = 128
QL = 1536
KVL = 512
NOPE = 128
ROPE = 64
VD = 128
BLK = 512
LEN = 256
TOKENS = 4096
BLOCKS = 13
SLOTS = 1
N_DP = 16
N_HEAD = 16


def draw_q_latent(key, part):
    key = jax.random.fold_in(key, 11)
    return jnp.clip(jax.random.normal(key, (TOKENS, QL), jnp.float32), -6.0, 6.0).astype(jnp.bfloat16)


def draw_kv_latent(key, part):
    key = jax.random.fold_in(key, 23)
    return jnp.clip(jax.random.normal(key, (TOKENS, KVL + ROPE), jnp.float32), -6.0, 6.0).astype(jnp.bfloat16)


def block_scale(stream_key, extent, cuts, smallest, high):
    loudness = 1.0
    for axis_at, blocks in cuts:
        heights = jax.random.uniform(jax.random.fold_in(jax.random.fold_in(stream_key, 6), axis_at), (blocks,), jnp.float32, smallest / len(cuts), high / len(cuts))
        loudness = loudness * jnp.repeat(jnp.exp(heights), extent[axis_at] // blocks).reshape((-1,) + (1,) * (len(extent) - 1 - axis_at))
    return loudness


def gaussian(rng, dims, scale, limit, shards=(), kind=jnp.bfloat16):
    result = scale * jax.random.normal(rng, dims, jnp.float32)
    if shards:
        result = result * block_scale(rng, dims, shards, -0.22, 0.18)
    return jnp.clip(result, -limit, limit).astype(kind)


def setup_inputs(seed: int = 0) -> dict:
    keys = jax.random.split(jax.random.key(seed), 6)
    q_latent = draw_q_latent(jax.random.fold_in(keys[5], 71), 0)
    kv_latent = draw_kv_latent(jax.random.fold_in(keys[5], 71), 0)
    q_up = gaussian(keys[2], (QL, HEADS * (NOPE + ROPE)), QL ** -0.5, 0.15625, ((0, 16), (1, 16)))
    kv_up = gaussian(keys[3], (KVL, HEADS * (NOPE + VD)), KVL ** -0.5, 0.25, ((0, 16), (1, 16)))
    out_grad = gaussian(keys[4], (TOKENS, HEADS * VD), 1.0, 6.0, ((0, 16), (1, 16)))
    return dict(q_latent=q_latent, kv_latent=kv_latent, q_up=q_up, kv_up=kv_up, out_grad=out_grad)


def reference(q_latent, kv_latent, q_up, kv_up, out_grad):
    qk_size = NOPE + ROPE
    kv_size = NOPE + VD
    scale = 1.0 / math.sqrt(qk_size)
    positions = jnp.arange(LEN)
    causal = positions[:, None] >= positions[None, :]
    kv_lat = kv_latent[:, :KVL]
    rope_key = kv_latent[:, KVL:]

    def one_head(carry, head):
        dq_total, dkv_total = carry
        w_query = lax.dynamic_slice_in_dim(q_up, (head * qk_size).astype(jnp.int32), qk_size, 1)
        w_keyval = lax.dynamic_slice_in_dim(kv_up, (head * kv_size).astype(jnp.int32), kv_size, 1)
        grad = lax.dynamic_slice_in_dim(out_grad, (head * VD).astype(jnp.int32), VD, 1)
        query = jnp.dot(q_latent, w_query, preferred_element_type=jnp.float32).astype(jnp.bfloat16)
        keyval = jnp.dot(kv_lat, w_keyval, preferred_element_type=jnp.float32).astype(jnp.bfloat16)
        key = jnp.concatenate([keyval[:, :NOPE], rope_key], axis=1)
        value = keyval[:, NOPE:]
        q_seq = query.reshape(N_DP, LEN, qk_size).astype(jnp.float32)
        k_seq = key.reshape(N_DP, LEN, qk_size).astype(jnp.float32)
        v_seq = value.reshape(N_DP, LEN, VD).astype(jnp.float32)
        g_seq = grad.reshape(N_DP, LEN, VD).astype(jnp.float32)
        scores = jnp.einsum('sqd,skd->sqk', q_seq, k_seq) * scale
        scores = jnp.where(causal[None], scores, -jnp.inf)
        weights = jnp.exp(scores)
        weights = weights / lax.optimization_barrier(jnp.sum(weights, axis=-1, keepdims=True))
        probs = lax.optimization_barrier(weights.astype(jnp.bfloat16)).astype(jnp.float32)
        attn_out = jnp.einsum('sqk,skd->sqd', probs, v_seq)
        delta = lax.optimization_barrier(jnp.sum(g_seq * attn_out, axis=-1, keepdims=True))
        dvalue = jnp.einsum('sqk,sqd->skd', probs, g_seq).astype(jnp.bfloat16)
        dprob = jnp.einsum('sqd,skd->sqk', g_seq, v_seq)
        dscore = (weights * (dprob - delta) * scale).astype(jnp.bfloat16)
        dscore = lax.optimization_barrier(dscore).astype(jnp.float32)
        dquery = jnp.einsum('sqk,skd->sqd', dscore, k_seq).astype(jnp.bfloat16).reshape(TOKENS, qk_size)
        dkey = jnp.einsum('sqk,sqd->skd', dscore, q_seq).astype(jnp.bfloat16).reshape(TOKENS, qk_size)
        dkeyval = jnp.concatenate([dkey[:, :NOPE], dvalue.reshape(TOKENS, VD)], axis=1)
        dq_total = dq_total + jnp.dot(dquery, w_query.T, preferred_element_type=jnp.float32)
        kv_term = jnp.concatenate([jnp.dot(dkeyval, w_keyval.T, preferred_element_type=jnp.float32), dkey[:, NOPE:].astype(jnp.float32)], axis=1)
        dkv_total = dkv_total + kv_term
        wq_grad = jnp.dot(q_latent.T, dquery, preferred_element_type=jnp.float32)
        wkv_grad = jnp.dot(kv_lat.T, dkeyval, preferred_element_type=jnp.float32)
        return ((dq_total, dkv_total), (wq_grad, wkv_grad))
    start = (jnp.zeros((TOKENS, QL), jnp.float32), jnp.zeros((TOKENS, KVL + ROPE), jnp.float32))
    (dq_total, dkv_total), (wq_stack, wkv_stack) = lax.scan(one_head, start, jnp.arange(HEADS, dtype=jnp.int32))
    q_wgrad = jnp.transpose(wq_stack, (1, 0, 2)).reshape(QL, HEADS * qk_size)
    kv_wgrad = jnp.transpose(wkv_stack, (1, 0, 2)).reshape(KVL, HEADS * kv_size)
    q_cols = HEADS // N_HEAD * qk_size
    kv_cols = HEADS // N_HEAD * kv_size

    def block_stack(matrix, rows, cols):
        pieces = matrix.reshape(rows // BLK, BLK, N_HEAD, cols // BLK, BLK)
        pieces = jnp.transpose(pieces, (2, 0, 3, 1, 4))
        return pieces.reshape(N_HEAD, rows // BLK * (cols // BLK), BLK, BLK)
    stacked = jnp.concatenate([block_stack(q_wgrad, QL, q_cols), block_stack(kv_wgrad, KVL, kv_cols)], axis=1)
    filler = jnp.zeros((N_HEAD, N_DP * SLOTS - BLOCKS, BLK, BLK), jnp.float32)
    grad_blocks = jnp.concatenate([stacked, filler], axis=1).reshape(N_HEAD * N_DP * SLOTS, BLK, BLK)
    left_gram = jnp.einsum('tic,tjc->tij', grad_blocks, grad_blocks, precision=lax.Precision.HIGHEST)
    right_gram = jnp.einsum('tci,tcj->tij', grad_blocks, grad_blocks, precision=lax.Precision.HIGHEST)
    return (dq_total.astype(jnp.bfloat16), dkv_total.astype(jnp.bfloat16), grad_blocks, left_gram, right_gram)
```

```python
import math

import jax
import jax.numpy as jnp
from jax import lax
from jax.experimental import pallas as pl
from jax.experimental.pallas import tpu as pltpu
from jax.sharding import PartitionSpec as P

KVL = 512
NOPE = 128
ROPE = 64
VD = 128
BLK = 512
QK = NOPE + ROPE
SCALE = 1.0 / math.sqrt(QK)
LOG2E = math.log2(math.e)

F32 = jnp.float32
BF16 = jnp.bfloat16


def dot(a, b, ca, cb):
    return lax.dot_general(a, b, (((ca,), (cb,)), ((), ())), preferred_element_type=F32)


def main_kernel(pos, ql, kl, lat0, lat1, og, w, dl, out_a, out_b, out_c, wq, wkv, lq, lk, rope, dq, dkv, kvt):
    member, group, core = pos[0], pos[1], pos[2]
    for d in range(16):
        for t in range(3):
            wq[96 * d : 96 * d + 96, 128 * t : 128 * t + 128] = w[d, 96 * t : 96 * t + 96, :]
        for t in range(4):
            wkv[32 * d : 32 * d + 32, 128 * t : 128 * t + 128] = w[d, 288 + 32 * t : 320 + 32 * t, :]
    lq[0:256, :] = ql[...]
    lk[0:256, :] = kl[:, :KVL]
    rope[0:256, :] = kl[:, KVL:]
    for i, lat in enumerate((lat0, lat1)):
        base = 128 * (core ^ i)
        for chip in range(8):
            for s in range(3):
                rows = pl.ds(pl.multiple_of(256 * (s + 1) + base + 16 * chip, 16), 16)
                at = 272 * s
                for t in range(12):
                    lq[rows, 128 * t : 128 * t + 128] = lat[chip, at + 16 * t : at + 16 * t + 16, :]
                for t in range(4):
                    lk[rows, 128 * t : 128 * t + 128] = lat[chip, at + 192 + 16 * t : at + 208 + 16 * t, :]
                rope[rows, :] = lat[chip, at + 256 : at + 272, :ROPE]

    causal = lax.broadcasted_iota(jnp.int32, (256, 256), 0) >= lax.broadcasted_iota(jnp.int32, (256, 256), 1)

    def sequence(s, carry):
        rows = pl.ds(pl.multiple_of(256 * s, 256), 256)
        who = member ^ s
        query = dot(lq[rows, :], wq[...], 1, 0)
        keyval = dot(lk[rows, :], wkv[...], 1, 0).astype(BF16)
        rope_key = rope[rows, :]
        rope_sum = jnp.zeros((256, ROPE), F32)
        dq_parts = []
        for h in range(2):
            q_h = query[:, QK * h : QK * h + QK].astype(BF16)
            key = jnp.concatenate([keyval[:, 256 * h : 256 * h + 128], rope_key], axis=1)
            value = keyval[:, 256 * h + 128 : 256 * h + 256]
            grad = og[who, :, 128 * h : 128 * h + 128]
            weights = jnp.where(causal, jnp.exp2(dot(q_h, key, 1, 1) * (SCALE * LOG2E)), 0.0)
            weights = weights / jnp.sum(weights, axis=1, keepdims=True)
            probs = weights.astype(BF16)
            dprob = dot(grad, value, 1, 1)
            delta = jnp.sum(probs.astype(F32) * dprob, axis=1, keepdims=True)
            dscore = (weights * (dprob - delta) * SCALE).astype(BF16)
            dvalue = dot(probs, grad, 0, 0).astype(BF16)
            dq_parts.append(dot(dscore, key, 1, 0))
            dkey = dot(dscore, q_h, 0, 0)
            dkv[rows, 256 * h : 256 * h + 128] = dkey[:, :NOPE].astype(BF16)
            dkv[rows, 256 * h + 128 : 256 * h + 256] = dvalue
            rope_sum = rope_sum + dkey[:, NOPE:].astype(BF16).astype(F32)
        dq[rows, :] = jnp.concatenate(dq_parts, axis=1).astype(BF16)
        q_term = dot(wq[...], dq[rows, :], 1, 1).astype(BF16)
        kvt[0:KVL, :] = dot(wkv[...], dkv[rows, :], 1, 1)
        kvt[KVL:, :] = rope_sum.T
        for h in range(16):
            side = (h % 2) ^ core
            dl[side, h // 2, who, 0:96, :] = q_term[96 * h : 96 * h + 96, :]
            piece = jnp.concatenate([kvt[36 * h : 36 * h + 36, :], jnp.zeros((12, 256), F32)], axis=0)
            dl[side, h // 2, who, 96:144, :] = piece.astype(BF16)
        return carry

    lax.fori_loop(0, 4, sequence, 0)

    for block in range(4):
        turn = (block - group + 4) % 4
        if block == 3:
            term = dot(lk[...], dkv[...], 0, 0).astype(BF16)
            out_a[turn] = term[:, :384]
            out_c[turn] = term[:, 384:]
            continue
        term = dot(lq[:, 512 * block : 512 * block + 512], dq[...], 0, 0).astype(BF16)

        @pl.when((member == 0) | (member == 3))
        def _():
            out_a[turn] = term

        @pl.when(member == 1)
        def _():
            out_a[turn, :, 0:256] = term[:, 128:]
            out_c[turn] = term[:, :128]

        @pl.when(member == 2)
        def _():
            out_b[turn] = term[:, :256]
            out_c[turn] = term[:, 256:]


def main_call(pos, ql, kl, lat0, lat1, og, w):
    vmem = pl.BlockSpec(memory_space=pltpu.VMEM)
    return pl.pallas_call(
        main_kernel,
        out_shape=(
            jax.ShapeDtypeStruct((2, 8, 4, 144, 256), BF16),
            jax.ShapeDtypeStruct((4, 512, 384), BF16),
            jax.ShapeDtypeStruct((4, 512, 256), BF16),
            jax.ShapeDtypeStruct((4, 512, 128), BF16),
        ),
        in_specs=[pl.BlockSpec(memory_space=pltpu.SMEM)] + [vmem] * 6,
        out_specs=(vmem,) * 4,
        scratch_shapes=[
            pltpu.VMEM((1536, 384), BF16),
            pltpu.VMEM((512, 512), BF16),
            pltpu.VMEM((1024, 1536), BF16),
            pltpu.VMEM((1024, 512), BF16),
            pltpu.VMEM((1024, ROPE), BF16),
            pltpu.VMEM((1024, 384), BF16),
            pltpu.VMEM((1024, 512), BF16),
            pltpu.VMEM((576, 256), F32),
        ],
        compiler_params=pltpu.CompilerParams(vmem_limit_bytes=48 * 1024 * 1024),
        cost_estimate=pl.CostEstimate(flops=6_300_000_000, bytes_accessed=16_000_000, transcendentals=524288),
        name="mla_backward",
    )(pos, ql, kl, lat0, lat1, og, w)


def gram_kernel(pos, *refs):
    terms, (grad, left, right) = refs[:12], refs[12:]
    owner = pos[0]
    is_q = owner < 9
    column = owner % 3

    def total(k):
        return sum(terms[3 * turn + k][...].astype(F32) for turn in range(4))

    @pl.when((is_q & (column == 0)) | ((owner >= 9) & (owner < 13)))
    def _():
        grad[:, 0:384] = total(0)
        grad[:, 384:512] = total(2)

    @pl.when(is_q & (column == 1))
    def _():
        grad[:, 0:256] = sum(terms[3 * turn][:, 0:256].astype(F32) for turn in range(4))
        grad[:, 256:512] = total(1)

    @pl.when(is_q & (column == 2))
    def _():
        grad[:, 0:128] = total(2)
        grad[:, 128:512] = total(0)

    @pl.when(owner >= 13)
    def _():
        grad[...] = jnp.zeros_like(grad)

    g = grad[...]
    highest = lax.Precision.HIGHEST
    left[...] = lax.dot_general(g, g, (((1,), (1,)), ((), ())), precision=highest, preferred_element_type=F32)
    right[...] = lax.dot_general(g, g, (((0,), (0,)), ((), ())), precision=highest, preferred_element_type=F32)


def gram_call(pos, terms):
    vmem = pl.BlockSpec(memory_space=pltpu.VMEM)
    block = jax.ShapeDtypeStruct((BLK, BLK), F32)
    return pl.pallas_call(
        gram_kernel,
        out_shape=(block, block, block),
        in_specs=[pl.BlockSpec(memory_space=pltpu.SMEM)] + [vmem] * 12,
        out_specs=(vmem,) * 3,
        compiler_params=pltpu.CompilerParams(vmem_limit_bytes=32 * 1024 * 1024),
        cost_estimate=pl.CostEstimate(flops=3_200_000_000, bytes_accessed=8_000_000, transcendentals=0),
        name="owner_grams",
    )(pos, *terms)


GROUPS = [[4 * a + m for m in range(4)] for a in range(4)]
SAME_CORE = [[2 * i + c for i in range(8)] for c in range(2)]


def term_routes(turn):
    route_a, route_b, route_c = [], [], []
    for a in range(4):
        block = (a + turn) % 4
        for m in range(4):
            here = 4 * a + m
            if block == 3:
                route_a.append((here, 9 + m))
                route_c.append((here, 9 + m))
                continue
            first = 3 * block
            if m == 0:
                route_a.append((here, first))
            elif m == 1:
                route_a.append((here, first + 1))
                route_c.append((here, first))
            elif m == 2:
                route_b.append((here, first + 1))
                route_c.append((here, first + 2))
            else:
                route_a.append((here, first + 2))
    return route_a, route_b, route_c


def per_device(q_latent, kv_latent, q_up, kv_up, out_grad):
    dp, head = lax.axis_index("dp"), lax.axis_index("head")
    member, group = dp % 4, dp // 4
    core, chip = head % 2, head // 2
    pos = jnp.stack([member, group, core, dp]).astype(jnp.int32)

    wq = q_up.reshape(96, 12, 128).transpose(1, 0, 2).reshape(4, 288, 128)
    wk = kv_up.reshape(32, 16, 128).transpose(1, 0, 2).reshape(4, 128, 128)
    w = jnp.concatenate([wq, wk], axis=1)
    w = jnp.broadcast_to(w[None], (4, 4, 416, 128)).reshape(16, 416, 128)

    row = 16 * (8 * core + chip)
    q_rows = lax.dynamic_slice_in_dim(q_latent, row, 16, 0)
    kv_rows = jnp.pad(lax.dynamic_slice_in_dim(kv_latent, row, 16, 0), ((0, 0), (0, 64)))
    piece = jnp.concatenate([q_rows, kv_rows], axis=1).reshape(16, 17, 128).transpose(1, 0, 2).reshape(272, 128)
    others = [lax.ppermute(piece, "dp", [(i, i ^ s) for i in range(16)]) for s in (1, 2, 3)]
    others = jnp.broadcast_to(jnp.concatenate(others, axis=0)[None], (8, 816, 128))
    lat0 = lax.all_to_all(others, "head", 0, 0, tiled=True, axis_index_groups=SAME_CORE)
    lat1 = lax.ppermute(lat0, "head", [(i, i ^ 1) for i in range(16)])

    og = out_grad.reshape(256, 4, 256).transpose(1, 0, 2)
    og = lax.all_to_all(og, "dp", 0, 0, tiled=True, axis_index_groups=GROUPS)

    w = lax.all_to_all(w, "dp", 0, 0, tiled=True)

    dl, out_a, out_b, out_c = main_call(pos, q_latent, kv_latent, lat0, lat1, og, w)

    terms = []
    for turn in range(4):
        for out, route in zip((out_a, out_b, out_c), term_routes(turn)):
            terms.append(lax.ppermute(out[turn], "dp", route))

    given = lax.ppermute(dl[1], "head", [(i, i ^ 1) for i in range(16)])
    dl = (dl[0].astype(F32) + given.astype(F32)).astype(BF16)
    dl = lax.all_to_all(dl, "head", 0, 0, tiled=True, axis_index_groups=SAME_CORE)
    dl = jnp.sum(dl.astype(F32), axis=0).astype(BF16)
    dl = lax.all_to_all(dl, "dp", 0, 0, tiled=True, axis_index_groups=GROUPS)
    dl = jnp.sum(dl.astype(F32), axis=0)
    d_q = dl[:96].T.astype(BF16)
    d_kv = dl[96:132].T.astype(BF16)

    owned, left, right = gram_call(pos[3:], terms)
    return d_q, d_kv, owned[None], left[None], right[None]


def solution(mesh):
    return jax.shard_map(
        per_device,
        mesh=mesh,
        in_specs=(P("dp", None), P("dp", None), P("dp", "head"), P("dp", "head"), P("dp", "head")),
        out_specs=(
            P("dp", "head"),
            P("dp", "head"),
            P(("head", "dp"), None, None),
            P(("head", "dp"), None, None),
            P(("head", "dp"), None, None),
        ),
        check_vma=False,
    )
```

```python
import math

import jax
import jax.numpy as jnp
from jax import lax
from jax.experimental import pallas as pl
from jax.experimental.pallas import tpu as pltpu
from jax.sharding import PartitionSpec as P

KVL = 512
NOPE = 128
ROPE = 64
VD = 128
BLK = 512
QK = NOPE + ROPE
SCALE = 1.0 / math.sqrt(QK)
LOG2E = math.log2(math.e)

F32 = jnp.float32
BF16 = jnp.bfloat16
WHOLE = 60


def dot(a, b, ca, cb):
    return lax.dot_general(a, b, (((ca,), (cb,)), ((), ())), preferred_element_type=F32)


def send_kernel(
    pos, ql_in, klt_in, qu_in, ku_in, grad, send1, send2, send3, own_w, og0, og1, og2, og3, kl, ql, klt, qu, ku, sems
):
    core, chip, member = pos[0], pos[1], pos[2]
    rows = pl.ds(pl.multiple_of(128 * core + 16 * chip, 16), 16)
    pairs = [(qu_in, qu), (ku_in, ku), (klt_in, klt), (ql_in.at[rows], ql)]
    copies_in = [pltpu.make_async_copy(x, y, sems.at[i]) for i, (x, y) in enumerate(pairs)]
    copies = []
    for s, out in enumerate((og0, og1, og2, og3)):
        for h in range(2):
            columns = pl.ds(pl.multiple_of(256 * (member ^ s) + 128 * h, 128), 128)
            part = pl.ds(256 * h, 256)
            copies.append(pltpu.make_async_copy(grad.at[:, columns], out.at[part], sems.at[4 + 2 * s + h]))
    for copy in copies_in + copies:
        copy.start()
    for copy in copies_in:
        copy.wait()
    kl[...] = klt[...].T
    for s, out in enumerate((own_w, send1, send2, send3)):
        to = 272 if s else 0
        for t in range(3):
            columns = pl.ds(pl.multiple_of(384 * (member ^ s) + 128 * t, 128), 128)
            out[to + 96 * t : to + 96 * t + 96, :] = qu[:, columns]
        for t in range(4):
            columns = pl.ds(pl.multiple_of(512 * (member ^ s) + 128 * t, 128), 128)
            out[to + 288 + 32 * t : to + 320 + 32 * t, :] = ku[:, columns]
        if s == 0:
            continue
        for t in range(12):
            out[16 * t : 16 * t + 16, :] = ql[:, 128 * t : 128 * t + 128]
        for t in range(4):
            out[192 + 16 * t : 208 + 16 * t, :] = kl[rows, 128 * t : 128 * t + 128]
        out[256:272, :ROPE] = kl[rows, KVL:]
        out[256:272, ROPE:] = jnp.zeros((16, 128 - ROPE), BF16)
    for copy in copies:
        copy.wait()


def latent_kernel(pos, ql, kl, *refs):
    lats, outs, (lq, lk, rope, sems) = refs[:8], refs[8:11], refs[11:]
    core, chip = pos[0], pos[1]
    lq[0:256, :] = ql[...]
    lk[0:256, :] = kl[:, :KVL]
    rope[0:256, :] = kl[:, KVL:]
    copies = []
    for s in range(4):
        for side in range(2 if s else 0):
            base = 128 * (core ^ side)
            for step in range(4):
                lat = lats[4 * side + step]
                for y in range(2):
                    source = 2 * ((chip // 2 - step + 4) % 4) + ((chip % 2) ^ y)
                    rows = pl.ds(pl.multiple_of(256 * s + base + 16 * source, 16), 16)
                    at = 272 * (s - 1)
                    for t in range(12):
                        lq[rows, 128 * t : 128 * t + 128] = lat[y, at + 16 * t : at + 16 * t + 16, :]
                    for t in range(4):
                        lk[rows, 128 * t : 128 * t + 128] = lat[y, at + 192 + 16 * t : at + 208 + 16 * t, :]
                    rope[rows, :] = lat[y, at + 256 : at + 272, :ROPE]
        part = pl.ds(256 * s, 256)
        for i, (source, out) in enumerate(zip((lq, lk, rope), outs)):
            copies.append(pltpu.make_async_copy(source.at[part], out.at[part], sems.at[s, i]))
            copies[-1].start()
    for copy in copies:
        copy.wait()


def call(kernel, name, out_shape, vmem_mib, args, scratch=(), out_specs=None, in_specs=None, flops=0, size=0, scalars=False):
    vmem = pl.BlockSpec(memory_space=pltpu.VMEM)
    specs = [vmem] * len(args)
    if scalars:
        specs[0] = pl.BlockSpec(memory_space=pltpu.SMEM)
    return pl.pallas_call(
        kernel,
        out_shape=out_shape,
        in_specs=specs if in_specs is None else in_specs,
        out_specs=[vmem] * len(out_shape) if out_specs is None else out_specs,
        scratch_shapes=scratch,
        compiler_params=pltpu.CompilerParams(vmem_limit_bytes=vmem_mib * 1024 * 1024),
        cost_estimate=pl.CostEstimate(flops=flops, bytes_accessed=size, transcendentals=0),
        name=name,
    )(*args)


def main_kernel(
    pos, lq_in, lk_in, rope_in, og0, og1, og2, og3, w0, w1, w2, w3, w4, out, given_out, wq_out, wkv_out,
    lq, lk, rope, og, wq3, wkv3, dq, dkv, drope, term, wq2, wkv2, w, row_sems, sems,
):
    core, member, group = pos[0], pos[2], pos[3]
    starts, at = [], 0
    for i, piece in enumerate((w0, w1, w2, w3, w4)):
        starts.append(pltpu.make_async_copy(piece, w.at[pl.ds(at, piece.shape[0])], sems.at[i]))
        at += piece.shape[0]
    for copy in starts:
        copy.start()

    def row_copies(s):
        part = pl.ds(256 * s, 256)
        pairs = [(lq_in, lq), (lk_in, lk), (rope_in, rope)]
        copies = [pltpu.make_async_copy(x.at[part], y.at[part], row_sems.at[s, i]) for i, (x, y) in enumerate(pairs)]
        return copies + [pltpu.make_async_copy((og0, og1, og2, og3)[s], og.at[s], row_sems.at[s, 3])]

    rows_in = [row_copies(s) for s in range(4)]
    for copies in rows_in:
        for copy in copies:
            copy.start()
    for copy in starts:
        copy.wait()
    for copy in rows_in[0]:
        copy.wait()
    for j, a in enumerate((0, 3, 1, 2)):
        for i in range(4):
            d = 4 * ((group + a) % 4) + (member ^ i)
            for t in range(3):
                wq3[d, :, 128 * t : 128 * t + 128] = w[4 * j + i, 96 * t : 96 * t + 96, :]
            for t in range(4):
                wkv3[d, :, 128 * t : 128 * t + 128] = w[4 * j + i, 288 + 32 * t : 320 + 32 * t, :]
    wq, wkv = wq3[...].reshape(1536, 384), wkv3[...].reshape(512, 512)
    wide = wkv.astype(F32)
    for h in range(16):
        side = (h % 2) ^ core
        own = min(max(KVL - 36 * h, 0), 36)
        wq2[side, 96 * (h // 2) : 96 * (h // 2) + 96, :] = wq[96 * h : 96 * h + 96, :]
        piece = jnp.zeros((48, 512), F32)
        if own:
            piece = jnp.concatenate([wide[36 * h : 36 * h + own, :], piece[own:]], axis=0)
        wkv2[side, 48 * (h // 2) : 48 * (h // 2) + 48, :] = piece.astype(BF16)
    ends = [
        pltpu.make_async_copy(wq2.at[0], wq_out, sems.at[7]),
        pltpu.make_async_copy(wkv2.at[0], wkv_out, sems.at[8]),
    ]
    for i, (source, to, tiles) in enumerate(((wq2.at[1], 7680, 3), (wkv2.at[1], 9984, 4))):
        size = source.shape[0]
        for t in range(tiles):
            part = given_out.at[pl.ds(to + size * t, size)]
            ends.append(pltpu.make_async_copy(source.at[:, pl.ds(128 * t, 128)], part, sems.at[16 + 4 * i + t]))
    for copy in ends:
        copy.start()

    causal = lax.broadcasted_iota(jnp.int32, (256, 256), 0) >= lax.broadcasted_iota(jnp.int32, (256, 256), 1)

    for s in range(4):
        if s:
            for copy in rows_in[s]:
                copy.wait()
        rows = pl.ds(256 * s, 256)
        query = dot(lq[rows, :], wq, 1, 0)
        keyval = dot(lk[rows, :], wkv, 1, 0).astype(BF16)
        rope_key = rope[rows, :]
        rope_sum = jnp.zeros((256, ROPE), F32)
        dq_parts = []
        for h in range(2):
            q_h = query[:, QK * h : QK * h + QK].astype(BF16)
            key = jnp.concatenate([keyval[:, 256 * h : 256 * h + 128], rope_key], axis=1)
            value = keyval[:, 256 * h + 128 : 256 * h + 256]
            grad = og[s, 256 * h : 256 * h + 256, :]
            weights = jnp.where(causal, jnp.exp2(dot(q_h, key, 1, 1) * (SCALE * LOG2E)), 0.0)
            weights = weights / jnp.sum(weights, axis=1, keepdims=True)
            probs = weights.astype(BF16)
            dprob = dot(grad, value, 1, 1)
            delta = jnp.sum(probs.astype(F32) * dprob, axis=1, keepdims=True)
            dscore = (weights * (dprob - delta) * SCALE).astype(BF16)
            dvalue = dot(probs, grad, 0, 0).astype(BF16)
            dq_parts.append(dot(dscore, key, 1, 0))
            dkey = dot(dscore, q_h, 0, 0)
            dkv[rows, 256 * h : 256 * h + 128] = dkey[:, :NOPE].astype(BF16)
            dkv[rows, 256 * h + 128 : 256 * h + 256] = dvalue
            rope_sum = rope_sum + dkey[:, NOPE:].astype(BF16).astype(F32)
        dq[rows, :] = jnp.concatenate(dq_parts, axis=1).astype(BF16)
        drope[:, 256 * s : 256 * s + 256] = rope_sum.T.astype(BF16)
        to = 1920 * s
        for i, (source, size, tiles) in enumerate(((dq.at[rows], 256, 3), (dkv.at[rows], 256, 4), (drope, ROPE, 2))):
            for t in range(tiles):
                columns = pl.ds(128 * t if i < 2 else 256 * s + 128 * t, 128)
                part = given_out.at[pl.ds(to, size)]
                ends.append(pltpu.make_async_copy(source.at[:, columns], part, sems.at[24 + 9 * s + 4 * i - min(i, 1) + t]))
                ends[-1].start()
                to += size

    for block in (3, 0, 1, 2):
        if block == 3:
            value = dot(lk[...], dkv[...], 0, 0).astype(BF16)
        else:
            value = dot(lq[:, 512 * block : 512 * block + 512], dq[...], 0, 0).astype(BF16)
        tiles = value.shape[1] // 128
        for d in range(16):
            for t in range(tiles):
                term[d, 3 * block + t] = value[32 * d : 32 * d + 32, 128 * t : 128 * t + 128]
        part = pl.ds(3 * block, tiles)
        ends.append(pltpu.make_async_copy(term.at[:, part], out.at[:, part], sems.at[12 + block]))
        ends[-1].start()
    for copy in ends:
        copy.wait()


def main_call(*args):
    shape = jax.ShapeDtypeStruct
    hbm = pl.BlockSpec(memory_space=pltpu.HBM)
    return call(
        main_kernel,
        "mla_backward",
        (
            shape((16, 13, 32, 128), BF16),
            shape((11520, 128), BF16),
            shape((768, 384), BF16),
            shape((384, 512), BF16),
        ),
        WHOLE,
        args,
        scratch=[
            pltpu.VMEM((1024, 1536), BF16),
            pltpu.VMEM((1024, 512), BF16),
            pltpu.VMEM((1024, ROPE), BF16),
            pltpu.VMEM((4, 512, 128), BF16),
            pltpu.VMEM((16, 96, 384), BF16),
            pltpu.VMEM((16, 32, 512), BF16),
            pltpu.VMEM((1024, 384), BF16),
            pltpu.VMEM((1024, 512), BF16),
            pltpu.VMEM((ROPE, 1024), BF16),
            pltpu.VMEM((16, 13, 32, 128), BF16),
            pltpu.VMEM((2, 768, 384), BF16),
            pltpu.VMEM((2, 384, 512), BF16),
            pltpu.VMEM((16, 416, 128), BF16),
            pltpu.SemaphoreType.DMA((4, 4)),
            pltpu.SemaphoreType.DMA((64,)),
        ],
        in_specs=[pl.BlockSpec(memory_space=pltpu.SMEM)] + [hbm] * 12,
        out_specs=[hbm] * 4,
        flops=4_500_000_000,
        size=12_000_000,
    )


def latent_grad_kernel(pos, mine, other, w_other, wq, wkv, *outs):
    core, chip = pos[0], pos[1]

    def wide(ref, at, size, tiles):
        return jnp.concatenate([ref[at + size * t : at + size * t + size, :] for t in range(tiles)], axis=1)

    wq_other, wkv_other = wide(w_other, 0, 768, 3), wide(w_other, 2304, 384, 4)
    q_term = dot(wq[...], wide(mine, 0, 256, 3), 1, 1) + dot(wq_other, wide(other, 0, 256, 3), 1, 1)
    kv_term = dot(wkv[...], wide(mine, 768, 256, 4), 1, 1) + dot(wkv_other, wide(other, 768, 256, 4), 1, 1)
    rotated = wide(mine, 1792, ROPE, 2).astype(F32) + wide(other, 1792, ROPE, 2).astype(F32)
    tail = jnp.zeros((48, 256), F32)
    on_0 = jnp.concatenate([tail[:8], rotated[:28], tail[36:]], axis=0)
    on_1 = jnp.concatenate([rotated[28:], tail[36:]], axis=0)
    last = kv_term[336:384] + jnp.where(core == 0, on_0, on_1)
    q_term = q_term.astype(BF16)
    kv_term = jnp.concatenate([kv_term[:336], last], axis=0).astype(BF16)
    for x in range(4):
        for y in range(2):
            h = 2 * x + y
            to_x, to_y = (x - chip // 2 + 4) % 4, y ^ (chip % 2)
            for k in range(4):

                @pl.when(to_x == k)
                def _():
                    outs[k][to_y, 0, 0:96, :] = q_term[96 * h : 96 * h + 96, :]
                    outs[k][to_y, 0, 96:144, :] = kv_term[48 * h : 48 * h + 48, :]


def latent_grad_call(pos, mine, other, wq, wkv):
    def whole(x):
        return pl.BlockSpec(x.shape, lambda s: (0, 0))

    sequence = pl.BlockSpec((1920, 128), lambda s: (s, 0))
    return pl.pallas_call(
        latent_grad_kernel,
        out_shape=[jax.ShapeDtypeStruct((2, 4, 144, 256), BF16)] * 4,
        grid=(4,),
        in_specs=[pl.BlockSpec(memory_space=pltpu.SMEM)]
        + [sequence, sequence, pl.BlockSpec((3840, 128), lambda s: (2, 0)), whole(wq), whole(wkv)],
        out_specs=[pl.BlockSpec((2, 1, 144, 256), lambda s: (0, s, 0, 0))] * 4,
        compiler_params=pltpu.CompilerParams(vmem_limit_bytes=WHOLE * 1024 * 1024),
        cost_estimate=pl.CostEstimate(flops=1_800_000_000, bytes_accessed=12_000_000, transcendentals=0),
        name="latent_grads",
    )(pos, mine, other, other, wq, wkv)


def strip_kernel(terms, strips):
    def summed(m, p):
        return sum(terms[4 * a + m, p].astype(F32) for a in range(4)).astype(BF16)

    for block in range(16):
        for u in range(4):
            if block < 9:
                column = 4 * (block % 3) + u
                strips[block, u] = summed(column // 3, 3 * (block // 3) + column % 3)
            elif block < 13:
                strips[block, u] = summed(block - 9, 9 + u)
            else:
                strips[block, u] = jnp.zeros((32, 128), BF16)


def gram_kernel(strips, grad, left, right):
    for d in range(16):
        for u in range(4):
            grad[32 * d : 32 * d + 32, 128 * u : 128 * u + 128] = strips[d, u].astype(F32)
    g = grad[...]
    highest = lax.Precision.HIGHEST
    left[...] = lax.dot_general(g, g, (((1,), (1,)), ((), ())), precision=highest, preferred_element_type=F32)
    right[...] = lax.dot_general(g, g, (((0,), (0,)), ((), ())), precision=highest, preferred_element_type=F32)


PARTNER = [[(i, i ^ s) for i in range(16)] for s in range(4)]
GROUP_UP = [(i, (i + 4) % 16) for i in range(16)]
GROUP_DOWN = [(i, (i + 12) % 16) for i in range(16)]
OTHER_CORE = [(i, i ^ 1) for i in range(16)]
ACROSS_Y = [(i, i ^ 2) for i in range(16)]
ALONG_X = [[(i, (i + 4 * k) % 16) for i in range(16)] for k in range(4)]


def per_device(q_latent, kv_latent, q_up, kv_up, out_grad):
    dp, head = lax.axis_index("dp"), lax.axis_index("head")
    member = dp % 4
    core, chip = head % 2, head // 2
    pos = jnp.stack([core, chip, member, dp // 4]).astype(jnp.int32)
    shape = jax.ShapeDtypeStruct
    vmem, hbm = pl.BlockSpec(memory_space=pltpu.VMEM), pl.BlockSpec(memory_space=pltpu.HBM)

    send, grad = shape((688, 128), BF16), shape((512, 128), BF16)
    *sends, own_w, og0, og1, og2, og3, kl = call(
        send_kernel,
        "send_rows",
        (send,) * 3 + (shape((416, 128), BF16),) + (grad,) * 4 + (shape((256, 576), BF16),),
        WHOLE,
        (pos, q_latent, kv_latent.T, q_up, kv_up, out_grad),
        scratch=[
            pltpu.VMEM((16, 1536), BF16),
            pltpu.VMEM((576, 256), BF16),
            pltpu.VMEM((96, 1536), BF16),
            pltpu.VMEM((32, 2048), BF16),
            pltpu.SemaphoreType.DMA((12,)),
        ],
        in_specs=[pl.BlockSpec(memory_space=pltpu.SMEM)] + [hbm] * 5,
        size=4_000_000,
        scalars=True,
    )
    parts = [lax.ppermute(sends[s - 1], "dp", PARTNER[s]) for s in (1, 2, 3)]
    w = jnp.stack([own_w] + [part[272:] for part in parts])
    from_down = lax.ppermute(w, "dp", GROUP_UP)
    from_up = lax.ppermute(w, "dp", GROUP_DOWN)
    far = [lax.ppermute(from_down[:2], "dp", GROUP_UP), lax.ppermute(from_up[2:], "dp", GROUP_DOWN)]
    ogs, _ = lax.optimization_barrier(((og1, og2, og3), (from_down, from_up)))
    ogs = [og0] + [lax.ppermute(ogs[s - 1], "dp", PARTNER[s]) for s in (1, 2, 3)]
    near = jnp.concatenate([part[:272] for part in parts], axis=0)
    near = jnp.stack([near, lax.ppermute(near, "head", ACROSS_Y)])
    lats = [near] + [lax.ppermute(near, "head", ALONG_X[k]) for k in (1, 2, 3)]
    lats, _ = lax.optimization_barrier((lats, (from_down, from_up)))
    lats = lats + [lax.ppermute(lat, "head", OTHER_CORE) for lat in lats]

    rows = (shape((1024, 1536), BF16), shape((1024, 512), BF16), shape((1024, ROPE), BF16))
    lq, lk, rope = call(
        latent_kernel,
        "latent_rows",
        rows,
        WHOLE,
        (pos, q_latent, kl, *lats),
        scratch=[pltpu.VMEM(x.shape, BF16) for x in rows] + [pltpu.SemaphoreType.DMA((4, 3))],
        out_specs=[hbm] * 3,
        size=9_000_000,
        scalars=True,
    )
    terms, mine, wq, wkv = main_call(pos, lq, lk, rope, *ogs, w, from_down, from_up, *far)
    terms = lax.all_to_all(terms, "dp", 0, 0, tiled=True)

    other = lax.ppermute(mine, "head", OTHER_CORE)
    parts = latent_grad_call(pos, mine, other, wq, wkv)
    parts = [parts[0]] + [lax.ppermute(parts[k], "head", ALONG_X[k]) for k in (1, 2, 3)]
    part = sum(p.astype(F32) for p in parts)
    across = lax.ppermute(part[1].astype(BF16), "head", ACROSS_Y)
    (strips,) = call(strip_kernel, "block_strips", (shape((16, 4, 32, 128), BF16),), 8, (terms,), size=3_000_000)
    part = (part[0] + across.astype(F32)).astype(BF16)
    parts = [part[0]] + [lax.ppermute(part[s], "dp", PARTNER[s]) for s in (1, 2, 3)]
    strips = lax.all_to_all(strips, "dp", 0, 0, tiled=True)
    block = shape((BLK, BLK), F32)
    owned, left, right = call(
        gram_kernel, "owner_grams", (block, block, block), 16, (strips,), flops=3_200_000_000, size=4_000_000
    )
    parts, _ = lax.optimization_barrier((parts, left))
    part = sum(p.astype(F32) for p in parts)
    d_q = part[:96].T.astype(BF16)
    d_kv = part[96:132].T.astype(BF16)
    return d_q, d_kv, owned[None], left[None], right[None]


def solution(mesh):
    return jax.shard_map(
        per_device,
        mesh=mesh,
        in_specs=(P("dp", None), P("dp", None), P("dp", "head"), P("dp", "head"), P("dp", "head")),
        out_specs=(
            P("dp", "head"),
            P("dp", "head"),
            P(("head", "dp"), None, None),
            P(("head", "dp"), None, None),
            P(("head", "dp"), None, None),
        ),
        check_vma=False,
    )
```

```python
import math

import jax
import jax.numpy as jnp
from jax import lax
from jax.experimental import pallas as pl
from jax.experimental.pallas import tpu as pltpu
from jax.sharding import PartitionSpec as P

KVL = 512
NOPE = 128
ROPE = 64
VD = 128
BLK = 512
QK = NOPE + ROPE
SCALE = 1.0 / math.sqrt(QK)
LOG2E = math.log2(math.e)

F32 = jnp.float32
BF16 = jnp.bfloat16
WHOLE = 60


def dot(a, b, ca, cb):
    return lax.dot_general(a, b, (((ca,), (cb,)), ((), ())), preferred_element_type=F32)


def send_kernel(
    pos, ql_in, klt_in, qu_in, ku_in, grad, send1, send2, send3, own_w, og0, og1, og2, og3, kl, ql, klt, qu, ku, sems
):
    core, chip, member = pos[0], pos[1], pos[2]
    rows = pl.ds(pl.multiple_of(128 * core + 16 * chip, 16), 16)
    pairs = [(qu_in, qu), (ku_in, ku), (klt_in, klt), (ql_in.at[rows], ql)]
    copies_in = [pltpu.make_async_copy(x, y, sems.at[i]) for i, (x, y) in enumerate(pairs)]
    copies = []
    for s, out in enumerate((og0, og1, og2, og3)):
        for h in range(2):
            columns = pl.ds(pl.multiple_of(256 * (member ^ s) + 128 * h, 128), 128)
            part = pl.ds(256 * h, 256)
            copies.append(pltpu.make_async_copy(grad.at[:, columns], out.at[part], sems.at[4 + 2 * s + h]))
    for copy in copies_in + copies:
        copy.start()
    for copy in copies_in:
        copy.wait()
    kl[...] = klt[...].T
    for s, out in enumerate((own_w, send1, send2, send3)):
        to = 272 if s else 0
        for t in range(3):
            columns = pl.ds(pl.multiple_of(384 * (member ^ s) + 128 * t, 128), 128)
            out[to + 96 * t : to + 96 * t + 96, :] = qu[:, columns]
        for t in range(4):
            columns = pl.ds(pl.multiple_of(512 * (member ^ s) + 128 * t, 128), 128)
            out[to + 288 + 32 * t : to + 320 + 32 * t, :] = ku[:, columns]
        if s == 0:
            continue
        for t in range(12):
            out[16 * t : 16 * t + 16, :] = ql[:, 128 * t : 128 * t + 128]
        for t in range(4):
            out[192 + 16 * t : 208 + 16 * t, :] = kl[rows, 128 * t : 128 * t + 128]
        out[256:272, :ROPE] = kl[rows, KVL:]
        out[256:272, ROPE:] = jnp.zeros((16, 128 - ROPE), BF16)
    for copy in copies:
        copy.wait()


def latent_kernel(pos, ql, kl, *refs):
    lats, outs, (lq, lk, rope, sems) = refs[:8], refs[8:11], refs[11:]
    core, chip = pos[0], pos[1]
    lq[0:256, :] = ql[...]
    lk[0:256, :] = kl[:, :KVL]
    rope[0:256, :] = kl[:, KVL:]
    copies = []
    for s in range(4):
        for side in range(2 if s else 0):
            base = 128 * (core ^ side)
            for step in range(4):
                lat = lats[4 * side + step]
                for y in range(2):
                    source = 2 * ((chip // 2 - step + 4) % 4) + ((chip % 2) ^ y)
                    rows = pl.ds(pl.multiple_of(256 * s + base + 16 * source, 16), 16)
                    at = 272 * (s - 1)
                    for t in range(12):
                        lq[rows, 128 * t : 128 * t + 128] = lat[y, at + 16 * t : at + 16 * t + 16, :]
                    for t in range(4):
                        lk[rows, 128 * t : 128 * t + 128] = lat[y, at + 192 + 16 * t : at + 208 + 16 * t, :]
                    rope[rows, :] = lat[y, at + 256 : at + 272, :ROPE]
        part = pl.ds(256 * s, 256)
        for i, (source, out) in enumerate(zip((lq, lk, rope), outs)):
            copies.append(pltpu.make_async_copy(source.at[part], out.at[part], sems.at[s, i]))
            copies[-1].start()
    for copy in copies:
        copy.wait()


def call(kernel, name, out_shape, vmem_mib, args, scratch=(), out_specs=None, in_specs=None, flops=0, size=0, scalars=False):
    vmem = pl.BlockSpec(memory_space=pltpu.VMEM)
    specs = [vmem] * len(args)
    if scalars:
        specs[0] = pl.BlockSpec(memory_space=pltpu.SMEM)
    return pl.pallas_call(
        kernel,
        out_shape=out_shape,
        in_specs=specs if in_specs is None else in_specs,
        out_specs=[vmem] * len(out_shape) if out_specs is None else out_specs,
        scratch_shapes=scratch,
        compiler_params=pltpu.CompilerParams(vmem_limit_bytes=vmem_mib * 1024 * 1024),
        cost_estimate=pl.CostEstimate(flops=flops, bytes_accessed=size, transcendentals=0),
        name=name,
    )(*args)


def project_kernel(
    pos, lq_in, lk_in, w0, w1, w2, w3, w4, query_out, keyval_out, wq_out, wkv_out, given_out,
    lq, lk, w, wq3, wkv3, query, keyval, wq2, wkv2, sems,
):
    core, member, group = pos[0], pos[2], pos[3]
    copies, at = [], 0
    for i, piece in enumerate((w0, w1, w2, w3, w4)):
        copies.append(pltpu.make_async_copy(piece, w.at[pl.ds(at, piece.shape[0])], sems.at[i]))
        at += piece.shape[0]
    rows_in = [pltpu.make_async_copy(lk_in, lk, sems.at[5]), pltpu.make_async_copy(lq_in, lq, sems.at[6])]
    for copy in copies + rows_in:
        copy.start()
    for copy in copies:
        copy.wait()
    for j, a in enumerate((0, 3, 1, 2)):
        for i in range(4):
            d = 4 * ((group + a) % 4) + (member ^ i)
            for t in range(3):
                wq3[d, :, 128 * t : 128 * t + 128] = w[4 * j + i, 96 * t : 96 * t + 96, :]
            for t in range(4):
                wkv3[d, :, 128 * t : 128 * t + 128] = w[4 * j + i, 288 + 32 * t : 320 + 32 * t, :]
    wq, wkv = wq3[...].reshape(1536, 384), wkv3[...].reshape(512, 512)
    rows_in[0].wait()
    keyval[...] = dot(lk[...], wkv, 1, 0).astype(BF16)
    ends = [pltpu.make_async_copy(keyval, keyval_out, sems.at[7])]
    ends[0].start()
    rows_in[1].wait()
    query[...] = dot(lq[...], wq, 1, 0).astype(BF16)
    wide = wkv.astype(F32)
    for h in range(16):
        side = (h % 2) ^ core
        own = min(max(KVL - 36 * h, 0), 36)
        wq2[side, 96 * (h // 2) : 96 * (h // 2) + 96, :] = wq[96 * h : 96 * h + 96, :]
        piece = jnp.zeros((48, 512), F32)
        if own:
            piece = jnp.concatenate([wide[36 * h : 36 * h + own, :], piece[own:]], axis=0)
        wkv2[side, 48 * (h // 2) : 48 * (h // 2) + 48, :] = piece.astype(BF16)
    last = [(query, query_out), (wq2.at[0], wq_out), (wkv2.at[0], wkv_out)]
    for source, to, tiles in ((wq2.at[1], 0, 3), (wkv2.at[1], 2304, 4)):
        size = source.shape[0]
        for t in range(tiles):
            last.append((source.at[:, pl.ds(128 * t, 128)], given_out.at[pl.ds(to + size * t, size)]))
    for i, (source, to) in enumerate(last):
        ends.append(pltpu.make_async_copy(source, to, sems.at[8 + i]))
        ends[-1].start()
    for copy in ends:
        copy.wait()


def project_call(*args):
    shape = jax.ShapeDtypeStruct
    hbm = pl.BlockSpec(memory_space=pltpu.HBM)
    shapes = [(1024, 384), (1024, 512), (768, 384), (384, 512), (3840, 128)]
    return call(
        project_kernel,
        "projections",
        [shape(x, BF16) for x in shapes],
        WHOLE,
        args,
        scratch=[
            pltpu.VMEM((1024, 1536), BF16),
            pltpu.VMEM((1024, 512), BF16),
            pltpu.VMEM((16, 416, 128), BF16),
            pltpu.VMEM((16, 96, 384), BF16),
            pltpu.VMEM((16, 32, 512), BF16),
            pltpu.VMEM((1024, 384), BF16),
            pltpu.VMEM((1024, 512), BF16),
            pltpu.VMEM((2, 768, 384), BF16),
            pltpu.VMEM((2, 384, 512), BF16),
            pltpu.SemaphoreType.DMA((18,)),
        ],
        in_specs=[pl.BlockSpec(memory_space=pltpu.SMEM)] + [hbm] * 7,
        out_specs=[hbm] * 5,
        flops=1_800_000_000,
        size=12_000_000,
    )


def main_kernel(
    lq_in, lk_in, rope_in, og0, og1, og2, og3, query_in, keyval_in, out, given_out,
    lq, lk, rope, og, dq, dkv, drope, term, row_sems, sems,
):
    whole = [pltpu.make_async_copy(lk_in, lk, sems.at[0]), pltpu.make_async_copy(lq_in, lq, sems.at[1])]
    rows_in = []
    for s, grad in enumerate((og0, og1, og2, og3)):
        rows = pl.ds(256 * s, 256)
        pairs = [(x.at[rows], y.at[rows]) for x, y in ((query_in, dq), (keyval_in, dkv), (rope_in, rope))]
        pairs.append((grad, og.at[s]))
        rows_in.append([pltpu.make_async_copy(x, y, row_sems.at[s, i]) for i, (x, y) in enumerate(pairs)])
        for copy in rows_in[s]:
            copy.start()
    for copy in whole:
        copy.start()

    causal = lax.broadcasted_iota(jnp.int32, (256, 256), 0) <= lax.broadcasted_iota(jnp.int32, (256, 256), 1)
    ends = []
    for s in range(4):
        rows = pl.ds(256 * s, 256)
        for copy in rows_in[s]:
            copy.wait()
        query, keyval, rope_key = dq[rows, :], dkv[rows, :], rope[rows, :]
        rope_sum = jnp.zeros((256, ROPE), F32)
        dq_parts = []
        for h in range(2):
            q_h = query[:, QK * h : QK * h + QK]
            key = jnp.concatenate([keyval[:, 256 * h : 256 * h + 128], rope_key], axis=1)
            value = keyval[:, 256 * h + 128 : 256 * h + 256]
            grad = og[s, 256 * h : 256 * h + 256, :]
            weights = jnp.where(causal, jnp.exp2(dot(key, q_h, 1, 1) * (SCALE * LOG2E)), 0.0)
            total = jnp.sum(weights, axis=0, keepdims=True)
            shrink = jnp.where(total > 2.0**100, 2.0**-100, 1.0)
            weights = (weights * shrink) * (1.0 / (total * shrink))
            probs = weights.astype(BF16)
            dprob = dot(value, grad, 1, 1)
            delta = jnp.sum(probs.astype(F32) * dprob, axis=0, keepdims=True)
            dscore = (weights * (dprob - delta) * SCALE).astype(BF16)
            dvalue = dot(probs, grad, 1, 0).astype(BF16)
            dkey = dot(dscore, q_h, 1, 0)
            dq_parts.append(dot(dscore, key, 0, 0))
            dkv[rows, 256 * h : 256 * h + 128] = dkey[:, :NOPE].astype(BF16)
            dkv[rows, 256 * h + 128 : 256 * h + 256] = dvalue
            rope_sum = rope_sum + dkey[:, NOPE:].astype(BF16).astype(F32)
        dq[rows, :] = jnp.concatenate(dq_parts, axis=1).astype(BF16)
        drope[:, 256 * s : 256 * s + 256] = rope_sum.T.astype(BF16)
        to = 1920 * s
        for i, (source, size, tiles) in enumerate(((dq.at[rows], 256, 3), (dkv.at[rows], 256, 4), (drope, ROPE, 2))):
            for t in range(tiles):
                columns = pl.ds(128 * t if i < 2 else 256 * s + 128 * t, 128)
                part = given_out.at[pl.ds(to, size)]
                ends.append(pltpu.make_async_copy(source.at[:, columns], part, sems.at[24 + 9 * s + 4 * i - min(i, 1) + t]))
                ends[-1].start()
                to += size

    for copy in whole:
        copy.wait()
    for block in (3, 0, 1, 2):
        if block == 3:
            value = dot(lk[...], dkv[...], 0, 0).astype(BF16)
        else:
            value = dot(lq[:, 512 * block : 512 * block + 512], dq[...], 0, 0).astype(BF16)
        tiles = value.shape[1] // 128
        for d in range(16):
            for t in range(tiles):
                term[d, 3 * block + t] = value[32 * d : 32 * d + 32, 128 * t : 128 * t + 128]
        part = pl.ds(3 * block, tiles)
        ends.append(pltpu.make_async_copy(term.at[:, part], out.at[:, part], sems.at[12 + block]))
        ends[-1].start()
    for copy in ends:
        copy.wait()


def main_call(*args):
    shape = jax.ShapeDtypeStruct
    hbm = pl.BlockSpec(memory_space=pltpu.HBM)
    return call(
        main_kernel,
        "mla_backward",
        [shape((16, 13, 32, 128), BF16), shape((7680, 128), BF16)],
        WHOLE,
        args,
        scratch=[
            pltpu.VMEM((1024, 1536), BF16),
            pltpu.VMEM((1024, 512), BF16),
            pltpu.VMEM((1024, ROPE), BF16),
            pltpu.VMEM((4, 512, 128), BF16),
            pltpu.VMEM((1024, 384), BF16),
            pltpu.VMEM((1024, 512), BF16),
            pltpu.VMEM((ROPE, 1024), BF16),
            pltpu.VMEM((16, 13, 32, 128), BF16),
            pltpu.SemaphoreType.DMA((4, 4)),
            pltpu.SemaphoreType.DMA((64,)),
        ],
        in_specs=[hbm] * 9,
        out_specs=[hbm] * 2,
        flops=2_700_000_000,
        size=12_000_000,
    )


def latent_grad_kernel(pos, mine, other, w_other, wq, wkv, *outs):
    core, chip = pos[0], pos[1]

    def wide(ref, at, size, tiles):
        return jnp.concatenate([ref[at + size * t : at + size * t + size, :] for t in range(tiles)], axis=1)

    wq_other, wkv_other = wide(w_other, 0, 768, 3), wide(w_other, 2304, 384, 4)
    q_term = dot(wq[...], wide(mine, 0, 256, 3), 1, 1) + dot(wq_other, wide(other, 0, 256, 3), 1, 1)
    kv_term = dot(wkv[...], wide(mine, 768, 256, 4), 1, 1) + dot(wkv_other, wide(other, 768, 256, 4), 1, 1)
    rotated = wide(mine, 1792, ROPE, 2).astype(F32) + wide(other, 1792, ROPE, 2).astype(F32)
    tail = jnp.zeros((48, 256), F32)
    on_0 = jnp.concatenate([tail[:8], rotated[:28], tail[36:]], axis=0)
    on_1 = jnp.concatenate([rotated[28:], tail[36:]], axis=0)
    last = kv_term[336:384] + jnp.where(core == 0, on_0, on_1)
    q_term = q_term.astype(BF16)
    kv_term = jnp.concatenate([kv_term[:336], last], axis=0).astype(BF16)
    along_x, (keep, give) = outs[:4], outs[4:]
    for x in range(4):
        for y in range(2):
            h = 2 * x + y
            to_x, to_y = (x - chip // 2 + 4) % 4, y ^ (chip % 2)
            q_piece, kv_piece = q_term[96 * h : 96 * h + 96, :], kv_term[48 * h : 48 * h + 48, :]
            for k in range(4):

                @pl.when((pl.program_id(0) < 2) & (to_x == k))
                def _():
                    along_x[k][to_y, 0, 0:96, :] = q_piece
                    along_x[k][to_y, 0, 96:144, :] = kv_piece

            for k, out in enumerate((keep, give)):

                @pl.when((pl.program_id(0) >= 2) & (to_y == k))
                def _():
                    out[to_x, 0, 0:96, :] = q_piece
                    out[to_x, 0, 96:144, :] = kv_piece


def latent_grad_call(pos, mine, other, w_other, wq, wkv):
    def whole(x):
        return pl.BlockSpec(x.shape, lambda s: (0, 0))

    sequence = pl.BlockSpec((1920, 128), lambda s: (s, 0))
    return pl.pallas_call(
        latent_grad_kernel,
        out_shape=[jax.ShapeDtypeStruct((2, 2, 144, 256), BF16)] * 4 + [jax.ShapeDtypeStruct((4, 2, 144, 256), BF16)] * 2,
        grid=(4,),
        in_specs=[pl.BlockSpec(memory_space=pltpu.SMEM)]
        + [sequence, sequence, whole(w_other), whole(wq), whole(wkv)],
        out_specs=[pl.BlockSpec((2, 1, 144, 256), lambda s: (0, jnp.minimum(s, 1), 0, 0))] * 4
        + [pl.BlockSpec((4, 1, 144, 256), lambda s: (0, jnp.maximum(s - 2, 0), 0, 0))] * 2,
        compiler_params=pltpu.CompilerParams(vmem_limit_bytes=WHOLE * 1024 * 1024),
        cost_estimate=pl.CostEstimate(flops=1_800_000_000, bytes_accessed=12_000_000, transcendentals=0),
        name="latent_grads",
    )(pos, mine, other, w_other, wq, wkv)


def strip_kernel(terms, strips):
    def summed(m, p):
        return sum(terms[4 * a + m, p].astype(F32) for a in range(4)).astype(BF16)

    for block in range(16):
        for u in range(4):
            if block < 9:
                column = 4 * (block % 3) + u
                strips[block, u] = summed(column // 3, 3 * (block // 3) + column % 3)
            elif block < 13:
                strips[block, u] = summed(block - 9, 9 + u)
            else:
                strips[block, u] = jnp.zeros((32, 128), BF16)


def gram_kernel(strips, grad_out, left_out, right_out, grad, left, right, sems):
    rows = [jnp.concatenate([strips[d, u] for u in range(4)], axis=1) for d in range(16)]
    g = jnp.concatenate(rows, axis=0)
    copies = []
    for i, (value, out) in enumerate(((grad, grad_out), (left, left_out), (right, right_out))):
        value[...] = g.astype(F32) if i == 0 else dot(g, g, 2 - i, 2 - i)
        copies.append(pltpu.make_async_copy(value, out, sems.at[i]))
        copies[-1].start()
    for copy in copies:
        copy.wait()


PARTNER = [[(i, i ^ s) for i in range(16)] for s in range(4)]
GROUP_UP = [(i, (i + 4) % 16) for i in range(16)]
GROUP_DOWN = [(i, (i + 12) % 16) for i in range(16)]
OTHER_CORE = [(i, i ^ 1) for i in range(16)]
ACROSS_Y = [(i, i ^ 2) for i in range(16)]
ALONG_X = [[(i, (i + 4 * k) % 16) for i in range(16)] for k in range(4)]


def per_device(q_latent, kv_latent, q_up, kv_up, out_grad):
    dp, head = lax.axis_index("dp"), lax.axis_index("head")
    member = dp % 4
    core, chip = head % 2, head // 2
    pos = jnp.stack([core, chip, member, dp // 4]).astype(jnp.int32)
    shape = jax.ShapeDtypeStruct
    vmem, hbm = pl.BlockSpec(memory_space=pltpu.VMEM), pl.BlockSpec(memory_space=pltpu.HBM)

    send, grad = shape((688, 128), BF16), shape((512, 128), BF16)
    *sends, own_w, og0, og1, og2, og3, kl = call(
        send_kernel,
        "send_rows",
        (send,) * 3 + (shape((416, 128), BF16),) + (grad,) * 4 + (shape((256, 576), BF16),),
        WHOLE,
        (pos, q_latent, kv_latent.T, q_up, kv_up, out_grad),
        scratch=[
            pltpu.VMEM((16, 1536), BF16),
            pltpu.VMEM((576, 256), BF16),
            pltpu.VMEM((96, 1536), BF16),
            pltpu.VMEM((32, 2048), BF16),
            pltpu.SemaphoreType.DMA((12,)),
        ],
        in_specs=[pl.BlockSpec(memory_space=pltpu.SMEM)] + [hbm] * 5,
        size=4_000_000,
        scalars=True,
    )
    parts = [lax.ppermute(sends[s - 1], "dp", PARTNER[s]) for s in (1, 2, 3)]
    w = jnp.stack([own_w] + [part[272:] for part in parts])
    from_down = lax.ppermute(w, "dp", GROUP_UP)
    from_up = lax.ppermute(w, "dp", GROUP_DOWN)
    far = [lax.ppermute(from_down[:2], "dp", GROUP_UP), lax.ppermute(from_up[2:], "dp", GROUP_DOWN)]
    ogs, _ = lax.optimization_barrier(((og1, og2, og3), (from_down, from_up)))
    ogs = [og0] + [lax.ppermute(ogs[s - 1], "dp", PARTNER[s]) for s in (1, 2, 3)]
    near = jnp.concatenate([part[:272] for part in parts], axis=0)
    near = jnp.stack([near, lax.ppermute(near, "head", ACROSS_Y)])
    lats = [near] + [lax.ppermute(near, "head", ALONG_X[k]) for k in (1, 2, 3)]
    lats, _ = lax.optimization_barrier((lats, (from_down, from_up)))
    lats = lats + [lax.ppermute(lat, "head", OTHER_CORE) for lat in lats]

    rows = (shape((1024, 1536), BF16), shape((1024, 512), BF16), shape((1024, ROPE), BF16))
    lq, lk, rope = call(
        latent_kernel,
        "latent_rows",
        rows,
        WHOLE,
        (pos, q_latent, kl, *lats),
        scratch=[pltpu.VMEM(x.shape, BF16) for x in rows] + [pltpu.SemaphoreType.DMA((4, 3))],
        out_specs=[hbm] * 3,
        size=9_000_000,
        scalars=True,
    )
    query, keyval, wq, wkv, w_given = project_call(pos, lq, lk, w, from_down, from_up, *far)
    w_other = lax.ppermute(w_given, "head", OTHER_CORE)
    terms, mine = main_call(lq, lk, rope, *ogs, query, keyval)
    terms = lax.all_to_all(terms, "dp", 0, 0, tiled=True)

    other = lax.ppermute(mine, "head", OTHER_CORE)
    *parts, keep, give = latent_grad_call(pos, mine, other, w_other, wq, wkv)
    given = lax.ppermute(give, "head", ACROSS_Y)
    parts = [parts[0]] + [lax.ppermute(parts[k], "head", ALONG_X[k]) for k in (1, 2, 3)]
    first = sum(p.astype(F32) for p in parts)
    first = first[0] + lax.ppermute(first[1].astype(BF16), "head", ACROSS_Y).astype(F32)
    parts = [(keep[k].astype(F32) + given[k].astype(F32)).astype(BF16) for k in range(4)]
    parts = [parts[0]] + [lax.ppermute(parts[k], "head", ALONG_X[k]) for k in (1, 2, 3)]
    second = sum(p.astype(F32) for p in parts)
    part = jnp.concatenate([first, second], axis=0).astype(BF16)
    parts = [part[0]] + [lax.ppermute(part[s], "dp", PARTNER[s]) for s in (1, 2, 3)]
    (strips,) = call(strip_kernel, "block_strips", (shape((16, 4, 32, 128), BF16),), 8, (terms,), size=3_000_000)
    strips = lax.all_to_all(strips, "dp", 0, 0, tiled=True)
    block = shape((BLK, BLK), F32)
    owned, left, right = call(
        gram_kernel,
        "owner_grams",
        (block, block, block),
        16,
        (strips,),
        scratch=[pltpu.VMEM((BLK, BLK), F32)] * 3 + [pltpu.SemaphoreType.DMA((3,))],
        out_specs=[hbm] * 3,
        flops=540_000_000,
        size=4_000_000,
    )
    *parts, left = lax.optimization_barrier((*parts, left))
    part = sum(p.astype(F32) for p in parts)
    d_q = part[:96].T.astype(BF16)
    d_kv = part[96:132].T.astype(BF16)
    return d_q, d_kv, owned[None], left[None], right[None]


def solution(mesh):
    return jax.shard_map(
        per_device,
        mesh=mesh,
        in_specs=(P("dp", None), P("dp", None), P("dp", "head"), P("dp", "head"), P("dp", "head")),
        out_specs=(
            P("dp", "head"),
            P("dp", "head"),
            P(("head", "dp"), None, None),
            P(("head", "dp"), None, None),
            P(("head", "dp"), None, None),
        ),
        check_vma=False,
    )
```

```python
import math

import jax
import jax.numpy as jnp
from jax import lax
from jax.experimental import pallas as pl
from jax.experimental.pallas import tpu as pltpu
from jax.sharding import PartitionSpec as P

KVL = 512
NOPE = 128
ROPE = 64
VD = 128
BLK = 512
QK = NOPE + ROPE
SCALE = 1.0 / math.sqrt(QK)
LOG2E = math.log2(math.e)

F32 = jnp.float32
BF16 = jnp.bfloat16
WHOLE = 60
VMEM_MAIN = 16


def dot(a, b, ca, cb):
    return lax.dot_general(a, b, (((ca,), (cb,)), ((), ())), preferred_element_type=F32)


def send_kernel(
    pos, ql_in, klt_in, qu_in, ku_in, grad, send1, send2, send3, own_w, og0, og1, og2, og3, kl, ql, klt, qu, ku, sems
):
    core, chip, member = pos[0], pos[1], pos[2]
    rows = pl.ds(pl.multiple_of(128 * core + 16 * chip, 16), 16)
    pairs = [(qu_in, qu), (ku_in, ku), (klt_in, klt), (ql_in.at[rows], ql)]
    copies_in = [pltpu.make_async_copy(x, y, sems.at[i]) for i, (x, y) in enumerate(pairs)]
    copies = []
    for s, out in enumerate((og0, og1, og2, og3)):
        for h in range(2):
            columns = pl.ds(pl.multiple_of(256 * (member ^ s) + 128 * h, 128), 128)
            part = pl.ds(256 * h, 256)
            copies.append(pltpu.make_async_copy(grad.at[:, columns], out.at[part], sems.at[4 + 2 * s + h]))
    for copy in copies_in + copies:
        copy.start()
    for copy in copies_in:
        copy.wait()
    kl[...] = klt[...].T
    for s, out in enumerate((own_w, send1, send2, send3)):
        to = 272 if s else 0
        for t in range(3):
            columns = pl.ds(pl.multiple_of(384 * (member ^ s) + 128 * t, 128), 128)
            out[to + 96 * t : to + 96 * t + 96, :] = qu[:, columns]
        for t in range(4):
            columns = pl.ds(pl.multiple_of(512 * (member ^ s) + 128 * t, 128), 128)
            out[to + 288 + 32 * t : to + 320 + 32 * t, :] = ku[:, columns]
        if s == 0:
            continue
        for t in range(12):
            out[16 * t : 16 * t + 16, :] = ql[:, 128 * t : 128 * t + 128]
        for t in range(4):
            out[192 + 16 * t : 208 + 16 * t, :] = kl[rows, 128 * t : 128 * t + 128]
        out[256:272, :ROPE] = kl[rows, KVL:]
        out[256:272, ROPE:] = jnp.zeros((16, 128 - ROPE), BF16)
    for copy in copies:
        copy.wait()


def latent_kernel(pos, ql, kl, *refs):
    lats, (lq, lk, rope) = refs[:8], refs[8:]
    core, chip = pos[0], pos[1]
    lq[0:256, :] = ql[...]
    lk[0:256, :] = kl[:, :KVL]
    rope[0:256, :] = kl[:, KVL:]
    for s in range(4):
        for side in range(2 if s else 0):
            base = 128 * (core ^ side)
            for step in range(4):
                lat = lats[4 * side + step]
                for y in range(2):
                    source = 2 * ((chip // 2 - step + 4) % 4) + ((chip % 2) ^ y)
                    rows = pl.ds(pl.multiple_of(256 * s + base + 16 * source, 16), 16)
                    at = 272 * (s - 1)
                    for t in range(12):
                        lq[rows, 128 * t : 128 * t + 128] = lat[y, at + 16 * t : at + 16 * t + 16, :]
                    for t in range(4):
                        lk[rows, 128 * t : 128 * t + 128] = lat[y, at + 192 + 16 * t : at + 208 + 16 * t, :]
                    rope[rows, :] = lat[y, at + 256 : at + 272, :ROPE]


def call(kernel, name, out_shape, vmem_mib, args, scratch=(), out_specs=None, in_specs=None, flops=0, size=0, scalars=False):
    vmem = pl.BlockSpec(memory_space=pltpu.VMEM)
    specs = [vmem] * len(args)
    if scalars:
        specs[0] = pl.BlockSpec(memory_space=pltpu.SMEM)
    return pl.pallas_call(
        kernel,
        out_shape=out_shape,
        in_specs=specs if in_specs is None else in_specs,
        out_specs=[vmem] * len(out_shape) if out_specs is None else out_specs,
        scratch_shapes=scratch,
        compiler_params=pltpu.CompilerParams(vmem_limit_bytes=vmem_mib * 1024 * 1024),
        cost_estimate=pl.CostEstimate(flops=flops, bytes_accessed=size, transcendentals=0),
        name=name,
    )(*args)


def project_kernel(
    pos, lq, lk, w0, w1, w2, w3, w4, query, keyval, wq_out, wkv_out, given_out, w, wq3, wkv3, wq2, wkv2, sems,
):
    core, member, group = pos[0], pos[2], pos[3]
    copies, at = [], 0
    for i, piece in enumerate((w0, w1, w2, w3, w4)):
        copies.append(pltpu.make_async_copy(piece, w.at[pl.ds(at, piece.shape[0])], sems.at[i]))
        at += piece.shape[0]
    for copy in copies:
        copy.start()
    for copy in copies:
        copy.wait()
    for j, a in enumerate((0, 3, 1, 2)):
        for i in range(4):
            d = 4 * ((group + a) % 4) + (member ^ i)
            for t in range(3):
                wq3[d, :, 128 * t : 128 * t + 128] = w[4 * j + i, 96 * t : 96 * t + 96, :]
            for t in range(4):
                wkv3[d, :, 128 * t : 128 * t + 128] = w[4 * j + i, 288 + 32 * t : 320 + 32 * t, :]
    wq, wkv = wq3[...].reshape(1536, 384), wkv3[...].reshape(512, 512)
    keyval[...] = dot(lk[...], wkv, 1, 0).astype(BF16)
    query[...] = dot(lq[...], wq, 1, 0).astype(BF16)
    wide = wkv.astype(F32)
    for h in range(16):
        side = (h % 2) ^ core
        own = min(max(KVL - 36 * h, 0), 36)
        wq2[side, 96 * (h // 2) : 96 * (h // 2) + 96, :] = wq[96 * h : 96 * h + 96, :]
        piece = jnp.zeros((48, 512), F32)
        if own:
            piece = jnp.concatenate([wide[36 * h : 36 * h + own, :], piece[own:]], axis=0)
        wkv2[side, 48 * (h // 2) : 48 * (h // 2) + 48, :] = piece.astype(BF16)
    last, ends = [(wq2.at[0], wq_out), (wkv2.at[0], wkv_out)], []
    for source, to, tiles in ((wq2.at[1], 0, 3), (wkv2.at[1], 2304, 4)):
        size = source.shape[0]
        for t in range(tiles):
            last.append((source.at[:, pl.ds(128 * t, 128)], given_out.at[pl.ds(to + size * t, size)]))
    for i, (source, to) in enumerate(last):
        ends.append(pltpu.make_async_copy(source, to, sems.at[8 + i]))
        ends[-1].start()
    for copy in ends:
        copy.wait()


def project_call(*args):
    shape = jax.ShapeDtypeStruct
    vmem, hbm = pl.BlockSpec(memory_space=pltpu.VMEM), pl.BlockSpec(memory_space=pltpu.HBM)
    shapes = [(768, 384), (384, 512), (3840, 128)]
    return call(
        project_kernel,
        "projections",
        [shape((1024, 384), BF16), shape((1024, 512), BF16)] + [pltpu.HBM(x, BF16) for x in shapes],
        24,
        args,
        scratch=[
            pltpu.VMEM((16, 416, 128), BF16),
            pltpu.VMEM((16, 96, 384), BF16),
            pltpu.VMEM((16, 32, 512), BF16),
            pltpu.VMEM((2, 768, 384), BF16),
            pltpu.VMEM((2, 384, 512), BF16),
            pltpu.SemaphoreType.DMA((18,)),
        ],
        in_specs=[pl.BlockSpec(memory_space=pltpu.SMEM)] + [vmem] * 2 + [hbm] * 5,
        out_specs=[vmem] * 2 + [hbm] * 3,
        flops=1_800_000_000,
        size=12_000_000,
    )


def main_kernel(
    lq, lk, rope, og0, og1, og2, og3, queries, keyvals, out, given_out, dq, dkv, drope, term, sems
):
    causal = lax.broadcasted_iota(jnp.int32, (256, 256), 0) <= lax.broadcasted_iota(jnp.int32, (256, 256), 1)
    ends = []
    for s in range(4):
        rows = pl.ds(256 * s, 256)
        query, keyval, rope_key = queries[rows, :], keyvals[rows, :], rope[rows, :]
        rope_sum = jnp.zeros((256, ROPE), F32)
        dq_parts = []
        for h in range(2):
            q_h = query[:, QK * h : QK * h + QK]
            key = jnp.concatenate([keyval[:, 256 * h : 256 * h + 128], rope_key], axis=1)
            value = keyval[:, 256 * h + 128 : 256 * h + 256]
            grad = (og0, og1, og2, og3)[s][256 * h : 256 * h + 256, :]
            weights = jnp.where(causal, jnp.exp2(dot(key, q_h, 1, 1) * (SCALE * LOG2E)), 0.0)
            total = jnp.sum(weights, axis=0, keepdims=True)
            shrink = jnp.where(total > 2.0**100, 2.0**-100, 1.0)
            weights = (weights * shrink) * (1.0 / (total * shrink))
            probs = weights.astype(BF16)
            dprob = dot(value, grad, 1, 1)
            delta = jnp.sum(probs.astype(F32) * dprob, axis=0, keepdims=True)
            dscore = (weights * (dprob - delta) * SCALE).astype(BF16)
            dvalue = dot(probs, grad, 1, 0).astype(BF16)
            dkey = dot(dscore, q_h, 1, 0)
            dq_parts.append(dot(dscore, key, 0, 0))
            dkv[rows, 256 * h : 256 * h + 128] = dkey[:, :NOPE].astype(BF16)
            dkv[rows, 256 * h + 128 : 256 * h + 256] = dvalue
            rope_sum = rope_sum + dkey[:, NOPE:].astype(BF16).astype(F32)
        dq[rows, :] = jnp.concatenate(dq_parts, axis=1).astype(BF16)
        drope[:, 256 * s : 256 * s + 256] = rope_sum.T.astype(BF16)
        to = 1920 * s
        for i, (source, size, tiles) in enumerate(((dq.at[rows], 256, 3), (dkv.at[rows], 256, 4), (drope, ROPE, 2))):
            for t in range(tiles):
                columns = pl.ds(128 * t if i < 2 else 256 * s + 128 * t, 128)
                part = given_out.at[pl.ds(to, size)]
                ends.append(pltpu.make_async_copy(source.at[:, columns], part, sems.at[24 + 9 * s + 4 * i - min(i, 1) + t]))
                ends[-1].start()
                to += size

    for block in (3, 0, 1, 2):
        if block == 3:
            value = dot(lk[...], dkv[...], 0, 0).astype(BF16)
        else:
            value = dot(lq[:, 512 * block : 512 * block + 512], dq[...], 0, 0).astype(BF16)
        tiles = value.shape[1] // 128
        for d in range(16):
            for t in range(tiles):
                term[d, 3 * block + t] = value[32 * d : 32 * d + 32, 128 * t : 128 * t + 128]
        part = pl.ds(3 * block, tiles)
        ends.append(pltpu.make_async_copy(term.at[:, part], out.at[:, part], sems.at[12 + block]))
        ends[-1].start()
    for copy in ends:
        copy.wait()


def main_call(*args):
    shape = jax.ShapeDtypeStruct
    hbm = pl.BlockSpec(memory_space=pltpu.HBM)
    return call(
        main_kernel,
        "mla_backward",
        [pltpu.HBM((16, 13, 32, 128), BF16), pltpu.HBM((7680, 128), BF16)],
        VMEM_MAIN,
        args,
        scratch=[
            pltpu.VMEM((1024, 384), BF16),
            pltpu.VMEM((1024, 512), BF16),
            pltpu.VMEM((ROPE, 1024), BF16),
            pltpu.VMEM((16, 13, 32, 128), BF16),
            pltpu.SemaphoreType.DMA((64,)),
        ],
        in_specs=None,
        out_specs=[hbm] * 2,
        flops=2_700_000_000,
        size=12_000_000,
    )


def latent_grad_kernel(pos, mine, other, w_other, wq, wkv, *outs):
    core, chip = pos[0], pos[1]

    def wide(ref, at, size, tiles):
        return jnp.concatenate([ref[at + size * t : at + size * t + size, :] for t in range(tiles)], axis=1)

    wq_other, wkv_other = wide(w_other, 0, 768, 3), wide(w_other, 2304, 384, 4)
    q_term = dot(wq[...], wide(mine, 0, 256, 3), 1, 1) + dot(wq_other, wide(other, 0, 256, 3), 1, 1)
    kv_term = dot(wkv[...], wide(mine, 768, 256, 4), 1, 1) + dot(wkv_other, wide(other, 768, 256, 4), 1, 1)
    rotated = wide(mine, 1792, ROPE, 2).astype(F32) + wide(other, 1792, ROPE, 2).astype(F32)
    tail = jnp.zeros((48, 256), F32)
    on_0 = jnp.concatenate([tail[:8], rotated[:28], tail[36:]], axis=0)
    on_1 = jnp.concatenate([rotated[28:], tail[36:]], axis=0)
    last = kv_term[336:384] + jnp.where(core == 0, on_0, on_1)
    q_term = q_term.astype(BF16)
    kv_term = jnp.concatenate([kv_term[:336], last], axis=0).astype(BF16)
    along_x, (keep, give) = outs[:4], outs[4:]
    for x in range(4):
        for y in range(2):
            h = 2 * x + y
            to_x, to_y = (x - chip // 2 + 4) % 4, y ^ (chip % 2)
            q_piece, kv_piece = q_term[96 * h : 96 * h + 96, :], kv_term[48 * h : 48 * h + 48, :]
            for k in range(4):

                @pl.when((pl.program_id(0) < 2) & (to_x == k))
                def _():
                    along_x[k][to_y, 0, 0:96, :] = q_piece
                    along_x[k][to_y, 0, 96:144, :] = kv_piece

            for k, out in enumerate((keep, give)):

                @pl.when((pl.program_id(0) >= 2) & (to_y == k))
                def _():
                    out[to_x, 0, 0:96, :] = q_piece
                    out[to_x, 0, 96:144, :] = kv_piece


def latent_grad_call(pos, mine, other, w_other, wq, wkv):
    def whole(x):
        return pl.BlockSpec(x.shape, lambda s: (0, 0))

    sequence = pl.BlockSpec((1920, 128), lambda s: (s, 0))
    return pl.pallas_call(
        latent_grad_kernel,
        out_shape=[jax.ShapeDtypeStruct((2, 2, 144, 256), BF16)] * 4 + [jax.ShapeDtypeStruct((4, 2, 144, 256), BF16)] * 2,
        grid=(4,),
        in_specs=[pl.BlockSpec(memory_space=pltpu.SMEM)]
        + [sequence, sequence, whole(w_other), whole(wq), whole(wkv)],
        out_specs=[pl.BlockSpec((2, 1, 144, 256), lambda s: (0, jnp.minimum(s, 1), 0, 0))] * 4
        + [pl.BlockSpec((4, 1, 144, 256), lambda s: (0, jnp.maximum(s - 2, 0), 0, 0))] * 2,
        compiler_params=pltpu.CompilerParams(vmem_limit_bytes=WHOLE * 1024 * 1024),
        cost_estimate=pl.CostEstimate(flops=1_800_000_000, bytes_accessed=12_000_000, transcendentals=0),
        name="latent_grads",
    )(pos, mine, other, w_other, wq, wkv)


def strip_kernel(terms, strips):
    def summed(m, p):
        return sum(terms[4 * a + m, p].astype(F32) for a in range(4)).astype(BF16)

    for block in range(16):
        for u in range(4):
            if block < 9:
                column = 4 * (block % 3) + u
                strips[block, u] = summed(column // 3, 3 * (block // 3) + column % 3)
            elif block < 13:
                strips[block, u] = summed(block - 9, 9 + u)
            else:
                strips[block, u] = jnp.zeros((32, 128), BF16)


def gram_kernel(strips, grad_out, left_out, right_out, grad, left, right, sems):
    rows = [jnp.concatenate([strips[d, u] for u in range(4)], axis=1) for d in range(16)]
    g = jnp.concatenate(rows, axis=0)
    copies = []
    for i, (value, out) in enumerate(((grad, grad_out), (left, left_out), (right, right_out))):
        value[...] = g.astype(F32) if i == 0 else dot(g, g, 2 - i, 2 - i)
        copies.append(pltpu.make_async_copy(value, out, sems.at[i]))
        copies[-1].start()
    for copy in copies:
        copy.wait()


PARTNER = [[(i, i ^ s) for i in range(16)] for s in range(4)]
GROUP_UP = [(i, (i + 4) % 16) for i in range(16)]
GROUP_DOWN = [(i, (i + 12) % 16) for i in range(16)]
OTHER_CORE = [(i, i ^ 1) for i in range(16)]
ACROSS_Y = [(i, i ^ 2) for i in range(16)]
ALONG_X = [[(i, (i + 4 * k) % 16) for i in range(16)] for k in range(4)]


def per_device(q_latent, kv_latent, q_up, kv_up, out_grad):
    dp, head = lax.axis_index("dp"), lax.axis_index("head")
    member = dp % 4
    core, chip = head % 2, head // 2
    pos = jnp.stack([core, chip, member, dp // 4]).astype(jnp.int32)
    shape = jax.ShapeDtypeStruct
    vmem, hbm = pl.BlockSpec(memory_space=pltpu.VMEM), pl.BlockSpec(memory_space=pltpu.HBM)

    send, grad = shape((688, 128), BF16), shape((512, 128), BF16)
    *sends, own_w, og0, og1, og2, og3, kl = call(
        send_kernel,
        "send_rows",
        (send,) * 3 + (shape((416, 128), BF16),) + (grad,) * 4 + (shape((256, 576), BF16),),
        WHOLE,
        (pos, q_latent, kv_latent.T, q_up, kv_up, out_grad),
        scratch=[
            pltpu.VMEM((16, 1536), BF16),
            pltpu.VMEM((576, 256), BF16),
            pltpu.VMEM((96, 1536), BF16),
            pltpu.VMEM((32, 2048), BF16),
            pltpu.SemaphoreType.DMA((12,)),
        ],
        in_specs=[pl.BlockSpec(memory_space=pltpu.SMEM)] + [hbm] * 5,
        size=4_000_000,
        scalars=True,
    )
    parts = [lax.ppermute(sends[s - 1], "dp", PARTNER[s]) for s in (1, 2, 3)]
    w = jnp.stack([own_w] + [part[272:] for part in parts])
    from_down = lax.ppermute(w, "dp", GROUP_UP)
    from_up = lax.ppermute(w, "dp", GROUP_DOWN)
    far = [lax.ppermute(from_down[:2], "dp", GROUP_UP), lax.ppermute(from_up[2:], "dp", GROUP_DOWN)]
    ogs, _ = lax.optimization_barrier(((og1, og2, og3), (from_down, from_up)))
    ogs = [og0] + [lax.ppermute(ogs[s - 1], "dp", PARTNER[s]) for s in (1, 2, 3)]
    near = jnp.concatenate([part[:272] for part in parts], axis=0)
    near = jnp.stack([near, lax.ppermute(near, "head", ACROSS_Y)])
    lats = [near] + [lax.ppermute(near, "head", ALONG_X[k]) for k in (1, 2, 3)]
    lats, _ = lax.optimization_barrier((lats, (from_down, from_up)))
    lats = lats + [lax.ppermute(lat, "head", OTHER_CORE) for lat in lats]

    rows = (shape((1024, 1536), BF16), shape((1024, 512), BF16), shape((1024, ROPE), BF16))
    lq, lk, rope = call(
        latent_kernel,
        "latent_rows",
        rows,
        20,
        (pos, q_latent, kl, *lats),
        size=9_000_000,
        scalars=True,
    )
    query, keyval, wq, wkv, w_given = project_call(pos, lq, lk, w, from_down, from_up, *far)
    w_other = lax.ppermute(w_given, "head", OTHER_CORE)
    terms, mine = main_call(lq, lk, rope, *ogs, query, keyval)
    terms = lax.all_to_all(terms, "dp", 0, 0, tiled=True)

    other = lax.ppermute(mine, "head", OTHER_CORE)
    *parts, keep, give = latent_grad_call(pos, mine, other, w_other, wq, wkv)
    given = lax.ppermute(give, "head", ACROSS_Y)
    parts = [parts[0]] + [lax.ppermute(parts[k], "head", ALONG_X[k]) for k in (1, 2, 3)]
    first = sum(p.astype(F32) for p in parts)
    first = first[0] + lax.ppermute(first[1].astype(BF16), "head", ACROSS_Y).astype(F32)
    parts = [(keep[k].astype(F32) + given[k].astype(F32)).astype(BF16) for k in range(4)]
    parts = [parts[0]] + [lax.ppermute(parts[k], "head", ALONG_X[k]) for k in (1, 2, 3)]
    second = sum(p.astype(F32) for p in parts)
    part = jnp.concatenate([first, second], axis=0).astype(BF16)
    parts = [part[0]] + [lax.ppermute(part[s], "dp", PARTNER[s]) for s in (1, 2, 3)]
    (strips,) = call(strip_kernel, "block_strips", (shape((16, 4, 32, 128), BF16),), 8, (terms,), size=3_000_000)
    strips = lax.all_to_all(strips, "dp", 0, 0, tiled=True)
    block = shape((BLK, BLK), F32)
    owned, left, right = call(
        gram_kernel,
        "owner_grams",
        (block, block, block),
        16,
        (strips,),
        scratch=[pltpu.VMEM((BLK, BLK), F32)] * 3 + [pltpu.SemaphoreType.DMA((3,))],
        out_specs=[hbm] * 3,
        flops=540_000_000,
        size=4_000_000,
    )
    *parts, left = lax.optimization_barrier((*parts, left))
    part = sum(p.astype(F32) for p in parts)
    d_q = part[:96].T.astype(BF16)
    d_kv = part[96:132].T.astype(BF16)
    return d_q, d_kv, owned[None], left[None], right[None]


def solution(mesh):
    return jax.shard_map(
        per_device,
        mesh=mesh,
        in_specs=(P("dp", None), P("dp", None), P("dp", "head"), P("dp", "head"), P("dp", "head")),
        out_specs=(
            P("dp", "head"),
            P("dp", "head"),
            P(("head", "dp"), None, None),
            P(("head", "dp"), None, None),
            P(("head", "dp"), None, None),
        ),
        check_vma=False,
    )
```

```python
import math

import jax
import jax.numpy as jnp
from jax import lax
from jax.experimental import pallas as pl
from jax.experimental.pallas import tpu as pltpu
from jax.sharding import PartitionSpec as P

KVL = 512
NOPE = 128
ROPE = 64
VD = 128
BLK = 512
QK = NOPE + ROPE
SCALE = 1.0 / math.sqrt(QK)
LOG2E = math.log2(math.e)

F32 = jnp.float32
BF16 = jnp.bfloat16
WHOLE = 60
VMEM_MAIN = 16


def dot(a, b, ca, cb):
    return lax.dot_general(a, b, (((ca,), (cb,)), ((), ())), preferred_element_type=F32)


def send_kernel(
    pos, ql_in, klt_in, qu_in, ku_in, grad, send1, send2, send3, own_w, og0, og1, og2, og3, kl, ql, klt, qu, ku, sems
):
    core, chip, member = pos[0], pos[1], pos[2]
    rows = pl.ds(pl.multiple_of(128 * core + 16 * chip, 16), 16)
    pairs = [(qu_in, qu), (ku_in, ku), (klt_in, klt), (ql_in.at[rows], ql)]
    copies_in = [pltpu.make_async_copy(x, y, sems.at[i]) for i, (x, y) in enumerate(pairs)]
    copies = []
    for s, out in enumerate((og0, og1, og2, og3)):
        for h in range(2):
            columns = pl.ds(pl.multiple_of(256 * (member ^ s) + 128 * h, 128), 128)
            part = pl.ds(256 * h, 256)
            copies.append(pltpu.make_async_copy(grad.at[:, columns], out.at[part], sems.at[4 + 2 * s + h]))
    for copy in copies_in + copies:
        copy.start()
    for copy in copies_in:
        copy.wait()
    kl[...] = klt[...].T
    for s, out in enumerate((own_w, send1, send2, send3)):
        to = 272 if s else 0
        for t in range(3):
            columns = pl.ds(pl.multiple_of(384 * (member ^ s) + 128 * t, 128), 128)
            out[to + 96 * t : to + 96 * t + 96, :] = qu[:, columns]
        for t in range(4):
            columns = pl.ds(pl.multiple_of(512 * (member ^ s) + 128 * t, 128), 128)
            out[to + 288 + 32 * t : to + 320 + 32 * t, :] = ku[:, columns]
        if s == 0:
            continue
        for t in range(12):
            out[16 * t : 16 * t + 16, :] = ql[:, 128 * t : 128 * t + 128]
        for t in range(4):
            out[192 + 16 * t : 208 + 16 * t, :] = kl[rows, 128 * t : 128 * t + 128]
        out[256:272, :ROPE] = kl[rows, KVL:]
        out[256:272, ROPE:] = jnp.zeros((16, 128 - ROPE), BF16)
    for copy in copies:
        copy.wait()


def latent_kernel(pos, ql, kl, *refs):
    lats, (lq, lk, rope) = refs[:8], refs[8:]
    core, chip = pos[0], pos[1]
    lq[0:256, :] = ql[...]
    lk[0:256, :] = kl[:, :KVL]
    rope[0:256, :] = kl[:, KVL:]
    for s in range(4):
        for side in range(2 if s else 0):
            base = 128 * (core ^ side)
            for step in range(4):
                lat = lats[4 * side + step]
                for y in range(2):
                    source = 2 * ((chip // 2 - step + 4) % 4) + ((chip % 2) ^ y)
                    rows = pl.ds(pl.multiple_of(256 * s + base + 16 * source, 16), 16)
                    at = 272 * (s - 1)
                    for t in range(12):
                        lq[rows, 128 * t : 128 * t + 128] = lat[y, at + 16 * t : at + 16 * t + 16, :]
                    for t in range(4):
                        lk[rows, 128 * t : 128 * t + 128] = lat[y, at + 192 + 16 * t : at + 208 + 16 * t, :]
                    rope[rows, :] = lat[y, at + 256 : at + 272, :ROPE]


def call(kernel, name, out_shape, vmem_mib, args, scratch=(), out_specs=None, in_specs=None, flops=0, size=0, scalars=False):
    vmem = pl.BlockSpec(memory_space=pltpu.VMEM)
    specs = [vmem] * len(args)
    if scalars:
        specs[0] = pl.BlockSpec(memory_space=pltpu.SMEM)
    return pl.pallas_call(
        kernel,
        out_shape=out_shape,
        in_specs=specs if in_specs is None else in_specs,
        out_specs=[vmem] * len(out_shape) if out_specs is None else out_specs,
        scratch_shapes=scratch,
        compiler_params=pltpu.CompilerParams(vmem_limit_bytes=vmem_mib * 1024 * 1024),
        cost_estimate=pl.CostEstimate(flops=flops, bytes_accessed=size, transcendentals=0),
        name=name,
    )(*args)


def project_kernel(
    pos, lq, lk, w0, w1, w2, w3, w4, query, keyval, wq_out, wkv_out, given_out, w, wq3, wkv3, wq2, wkv2, sems,
):
    core, member, group = pos[0], pos[2], pos[3]
    copies, at = [], 0
    for i, piece in enumerate((w0, w1, w2, w3, w4)):
        copies.append(pltpu.make_async_copy(piece, w.at[pl.ds(at, piece.shape[0])], sems.at[i]))
        at += piece.shape[0]
    for copy in copies:
        copy.start()
    for copy in copies:
        copy.wait()
    for j, a in enumerate((0, 3, 1, 2)):
        for i in range(4):
            d = 4 * ((group + a) % 4) + (member ^ i)
            for t in range(3):
                wq3[d, :, 128 * t : 128 * t + 128] = w[4 * j + i, 96 * t : 96 * t + 96, :]
            for t in range(4):
                wkv3[d, :, 128 * t : 128 * t + 128] = w[4 * j + i, 288 + 32 * t : 320 + 32 * t, :]
    wq, wkv = wq3[...].reshape(1536, 384), wkv3[...].reshape(512, 512)
    keyval[...] = dot(lk[...], wkv, 1, 0).astype(BF16)
    query[...] = dot(lq[...], wq, 1, 0).astype(BF16)
    wide = wkv.astype(F32)
    for h in range(16):
        side = (h % 2) ^ core
        own = min(max(KVL - 36 * h, 0), 36)
        wq2[side, 96 * (h // 2) : 96 * (h // 2) + 96, :] = wq[96 * h : 96 * h + 96, :]
        piece = jnp.zeros((48, 512), F32)
        if own:
            piece = jnp.concatenate([wide[36 * h : 36 * h + own, :], piece[own:]], axis=0)
        wkv2[side, 48 * (h // 2) : 48 * (h // 2) + 48, :] = piece.astype(BF16)
    last, ends = [(wq2.at[0], wq_out), (wkv2.at[0], wkv_out)], []
    for source, to, tiles in ((wq2.at[1], 0, 3), (wkv2.at[1], 2304, 4)):
        size = source.shape[0]
        for t in range(tiles):
            last.append((source.at[:, pl.ds(128 * t, 128)], given_out.at[pl.ds(to + size * t, size)]))
    for i, (source, to) in enumerate(last):
        ends.append(pltpu.make_async_copy(source, to, sems.at[8 + i]))
        ends[-1].start()
    for copy in ends:
        copy.wait()


def project_call(*args):
    shape = jax.ShapeDtypeStruct
    vmem, hbm = pl.BlockSpec(memory_space=pltpu.VMEM), pl.BlockSpec(memory_space=pltpu.HBM)
    shapes = [(768, 384), (384, 512), (3840, 128)]
    return call(
        project_kernel,
        "projections",
        [shape((1024, 384), BF16), shape((1024, 512), BF16)] + [pltpu.HBM(x, BF16) for x in shapes],
        24,
        args,
        scratch=[
            pltpu.VMEM((16, 416, 128), BF16),
            pltpu.VMEM((16, 96, 384), BF16),
            pltpu.VMEM((16, 32, 512), BF16),
            pltpu.VMEM((2, 768, 384), BF16),
            pltpu.VMEM((2, 384, 512), BF16),
            pltpu.SemaphoreType.DMA((18,)),
        ],
        in_specs=[pl.BlockSpec(memory_space=pltpu.SMEM)] + [vmem] * 2 + [hbm] * 5,
        out_specs=[vmem] * 2 + [hbm] * 3,
        flops=1_800_000_000,
        size=12_000_000,
    )


def main_kernel(
    lq, lk, rope, og0, og1, og2, og3, queries, keyvals, out, given_out, dq, dkv, drope, term, sems
):
    causal = lax.broadcasted_iota(jnp.int32, (256, 256), 0) <= lax.broadcasted_iota(jnp.int32, (256, 256), 1)
    ends = []
    for s in range(4):
        rows = pl.ds(256 * s, 256)
        query, keyval, rope_key = queries[rows, :], keyvals[rows, :], rope[rows, :]
        rope_sum = jnp.zeros((256, ROPE), F32)
        dq_parts = []
        for h in range(2):
            q_h = query[:, QK * h : QK * h + QK]
            key = jnp.concatenate([keyval[:, 256 * h : 256 * h + 128], rope_key], axis=1)
            value = keyval[:, 256 * h + 128 : 256 * h + 256]
            grad = (og0, og1, og2, og3)[s][256 * h : 256 * h + 256, :]
            weights = jnp.where(causal, jnp.exp2(dot(key, q_h, 1, 1) * (SCALE * LOG2E)), 0.0)
            total = jnp.sum(weights, axis=0, keepdims=True)
            shrink = jnp.where(total > 2.0**100, 2.0**-100, 1.0)
            weights = (weights * shrink) * (1.0 / (total * shrink))
            probs = weights.astype(BF16)
            dprob = dot(value, grad, 1, 1)
            delta = jnp.sum(probs.astype(F32) * dprob, axis=0, keepdims=True)
            dscore = (weights * (dprob - delta) * SCALE).astype(BF16)
            dvalue = dot(probs, grad, 1, 0).astype(BF16)
            dkey = dot(dscore, q_h, 1, 0)
            dq_parts.append(dot(dscore, key, 0, 0))
            dkv[rows, 256 * h : 256 * h + 128] = dkey[:, :NOPE].astype(BF16)
            dkv[rows, 256 * h + 128 : 256 * h + 256] = dvalue
            rope_sum = rope_sum + dkey[:, NOPE:].astype(BF16).astype(F32)
        dq[rows, :] = jnp.concatenate(dq_parts, axis=1).astype(BF16)
        drope[:, 256 * s : 256 * s + 256] = rope_sum.T.astype(BF16)
        to = 1920 * s
        for i, (source, size, tiles) in enumerate(((dq.at[rows], 256, 3), (dkv.at[rows], 256, 4), (drope, ROPE, 2))):
            for t in range(tiles):
                columns = pl.ds(128 * t if i < 2 else 256 * s + 128 * t, 128)
                part = given_out.at[pl.ds(to, size)]
                ends.append(pltpu.make_async_copy(source.at[:, columns], part, sems.at[24 + 9 * s + 4 * i - min(i, 1) + t]))
                ends[-1].start()
                to += size

    for block in (3, 0, 1, 2):
        if block == 3:
            value = dot(lk[...], dkv[...], 0, 0).astype(BF16)
        else:
            value = dot(lq[:, 512 * block : 512 * block + 512], dq[...], 0, 0).astype(BF16)
        tiles = value.shape[1] // 128
        for d in range(16):
            for t in range(tiles):
                term[d, 3 * block + t] = value[32 * d : 32 * d + 32, 128 * t : 128 * t + 128]
        part = pl.ds(3 * block, tiles)
        ends.append(pltpu.make_async_copy(term.at[:, part], out.at[:, part], sems.at[12 + block]))
        ends[-1].start()
    for copy in ends:
        copy.wait()


def main_call(*args):
    shape = jax.ShapeDtypeStruct
    hbm = pl.BlockSpec(memory_space=pltpu.HBM)
    return call(
        main_kernel,
        "mla_backward",
        [pltpu.HBM((16, 13, 32, 128), BF16), pltpu.HBM((7680, 128), BF16)],
        VMEM_MAIN,
        args,
        scratch=[
            pltpu.VMEM((1024, 384), BF16),
            pltpu.VMEM((1024, 512), BF16),
            pltpu.VMEM((ROPE, 1024), BF16),
            pltpu.VMEM((16, 13, 32, 128), BF16),
            pltpu.SemaphoreType.DMA((64,)),
        ],
        in_specs=None,
        out_specs=[hbm] * 2,
        flops=2_700_000_000,
        size=12_000_000,
    )


def latent_grad_kernel(pos, mine, other, w_other, wq, wkv, *outs):
    core, chip = pos[0], pos[1]

    def wide(ref, at, size, tiles):
        return jnp.concatenate([ref[at + size * t : at + size * t + size, :] for t in range(tiles)], axis=1)

    wq_other, wkv_other = wide(w_other, 0, 768, 3), wide(w_other, 2304, 384, 4)
    q_term = dot(wq[...], wide(mine, 0, 256, 3), 1, 1) + dot(wq_other, wide(other, 0, 256, 3), 1, 1)
    kv_term = dot(wkv[...], wide(mine, 768, 256, 4), 1, 1) + dot(wkv_other, wide(other, 768, 256, 4), 1, 1)
    rotated = wide(mine, 1792, ROPE, 2).astype(F32) + wide(other, 1792, ROPE, 2).astype(F32)
    tail = jnp.zeros((48, 256), F32)
    on_0 = jnp.concatenate([tail[:8], rotated[:28], tail[36:]], axis=0)
    on_1 = jnp.concatenate([rotated[28:], tail[36:]], axis=0)
    last = kv_term[336:384] + jnp.where(core == 0, on_0, on_1)
    q_term = q_term.astype(BF16)
    kv_term = jnp.concatenate([kv_term[:336], last], axis=0).astype(BF16)
    along_x, (keep, give) = outs[:4], outs[4:]
    for x in range(4):
        for y in range(2):
            h = 2 * x + y
            to_x, to_y = (x - chip // 2 + 4) % 4, y ^ (chip % 2)
            q_piece, kv_piece = q_term[96 * h : 96 * h + 96, :], kv_term[48 * h : 48 * h + 48, :]
            for k in range(4):

                @pl.when((pl.program_id(0) < 2) & (to_x == k))
                def _():
                    along_x[k][to_y, 0, 0:96, :] = q_piece
                    along_x[k][to_y, 0, 96:144, :] = kv_piece

            for k, out in enumerate((keep, give)):

                @pl.when((pl.program_id(0) >= 2) & (to_y == k))
                def _():
                    out[to_x, 0, 0:96, :] = q_piece
                    out[to_x, 0, 96:144, :] = kv_piece


def latent_grad_call(pos, mine, other, w_other, wq, wkv):
    def whole(x):
        return pl.BlockSpec(x.shape, lambda s: (0, 0))

    sequence = pl.BlockSpec((1920, 128), lambda s: (s, 0))
    return pl.pallas_call(
        latent_grad_kernel,
        out_shape=[jax.ShapeDtypeStruct((2, 2, 144, 256), BF16)] * 4 + [jax.ShapeDtypeStruct((4, 2, 144, 256), BF16)] * 2,
        grid=(4,),
        in_specs=[pl.BlockSpec(memory_space=pltpu.SMEM)]
        + [sequence, sequence, whole(w_other), whole(wq), whole(wkv)],
        out_specs=[pl.BlockSpec((2, 1, 144, 256), lambda s: (0, jnp.minimum(s, 1), 0, 0))] * 4
        + [pl.BlockSpec((4, 1, 144, 256), lambda s: (0, jnp.maximum(s - 2, 0), 0, 0))] * 2,
        compiler_params=pltpu.CompilerParams(vmem_limit_bytes=WHOLE * 1024 * 1024),
        cost_estimate=pl.CostEstimate(flops=1_800_000_000, bytes_accessed=12_000_000, transcendentals=0),
        name="latent_grads",
    )(pos, mine, other, w_other, wq, wkv)


def strip_kernel(terms, strips):
    def summed(m, p):
        return sum(terms[4 * a + m, p].astype(F32) for a in range(4)).astype(BF16)

    for block in range(16):
        for u in range(4):
            if block < 9:
                column = 4 * (block % 3) + u
                strips[block, u] = summed(column // 3, 3 * (block // 3) + column % 3)
            elif block < 13:
                strips[block, u] = summed(block - 9, 9 + u)
            else:
                strips[block, u] = jnp.zeros((32, 128), BF16)


def gram_kernel(strips, grad_out, left_out, right_out, grad, left, right, sems):
    rows = [jnp.concatenate([strips[d, u] for u in range(4)], axis=1) for d in range(16)]
    g = jnp.concatenate(rows, axis=0)
    copies = []
    for i, (value, out) in enumerate(((grad, grad_out), (left, left_out), (right, right_out))):
        value[...] = g.astype(F32) if i == 0 else dot(g, g, 2 - i, 2 - i)
        copies.append(pltpu.make_async_copy(value, out, sems.at[i]))
        copies[-1].start()
    for copy in copies:
        copy.wait()


PARTNER = [[(i, i ^ s) for i in range(16)] for s in range(4)]
GROUP_UP = [(i, (i + 4) % 16) for i in range(16)]
GROUP_DOWN = [(i, (i + 12) % 16) for i in range(16)]
OTHER_CORE = [(i, i ^ 1) for i in range(16)]
ACROSS_Y = [(i, i ^ 2) for i in range(16)]
ALONG_X = [[(i, (i + 4 * k) % 16) for i in range(16)] for k in range(4)]


def per_device(q_latent, kv_latent, q_up, kv_up, out_grad):
    dp, head = lax.axis_index("dp"), lax.axis_index("head")
    member = dp % 4
    core, chip = head % 2, head // 2
    pos = jnp.stack([core, chip, member, dp // 4]).astype(jnp.int32)
    shape = jax.ShapeDtypeStruct
    vmem, hbm = pl.BlockSpec(memory_space=pltpu.VMEM), pl.BlockSpec(memory_space=pltpu.HBM)

    send, grad = shape((688, 128), BF16), shape((512, 128), BF16)
    *sends, own_w, og0, og1, og2, og3, kl = call(
        send_kernel,
        "send_rows",
        (send,) * 3 + (shape((416, 128), BF16),) + (grad,) * 4 + (shape((256, 576), BF16),),
        WHOLE,
        (pos, q_latent, kv_latent.T, q_up, kv_up, out_grad),
        scratch=[
            pltpu.VMEM((16, 1536), BF16),
            pltpu.VMEM((576, 256), BF16),
            pltpu.VMEM((96, 1536), BF16),
            pltpu.VMEM((32, 2048), BF16),
            pltpu.SemaphoreType.DMA((12,)),
        ],
        in_specs=[pl.BlockSpec(memory_space=pltpu.SMEM)] + [hbm] * 5,
        size=4_000_000,
        scalars=True,
    )
    parts = [lax.ppermute(sends[s - 1], "dp", PARTNER[s]) for s in (1, 2, 3)]
    w = jnp.stack([own_w] + [part[272:] for part in parts])
    from_down = lax.ppermute(w, "dp", GROUP_UP)
    from_up = lax.ppermute(w, "dp", GROUP_DOWN)
    far = [lax.ppermute(from_down[:2], "dp", GROUP_UP), lax.ppermute(from_up[2:], "dp", GROUP_DOWN)]
    ogs, _ = lax.optimization_barrier(((og1, og2, og3), (from_down, from_up)))
    ogs = [og0] + [lax.ppermute(ogs[s - 1], "dp", PARTNER[s]) for s in (1, 2, 3)]
    near = jnp.concatenate([part[:272] for part in parts], axis=0)
    near = jnp.stack([near, lax.ppermute(near, "head", ACROSS_Y)])
    lats = [near] + [lax.ppermute(near, "head", ALONG_X[k]) for k in (1, 2, 3)]
    lats, far = lax.optimization_barrier((lats, far))
    lats = lats + [lax.ppermute(lat, "head", OTHER_CORE) for lat in lats]

    rows = (shape((1024, 1536), BF16), shape((1024, 512), BF16), shape((1024, ROPE), BF16))
    lq, lk, rope = call(
        latent_kernel,
        "latent_rows",
        rows,
        20,
        (pos, q_latent, kl, *lats),
        size=9_000_000,
        scalars=True,
    )
    query, keyval, wq, wkv, w_given = project_call(pos, lq, lk, w, from_down, from_up, *far)
    w_other = lax.ppermute(w_given, "head", OTHER_CORE)
    terms, mine = main_call(lq, lk, rope, *ogs, query, keyval)
    terms = lax.all_to_all(terms, "dp", 0, 0, tiled=True)

    other = lax.ppermute(mine, "head", OTHER_CORE)
    *parts, keep, give = latent_grad_call(pos, mine, other, w_other, wq, wkv)
    given = lax.ppermute(give, "head", ACROSS_Y)
    parts = [parts[0]] + [lax.ppermute(parts[k], "head", ALONG_X[k]) for k in (1, 2, 3)]
    first = sum(p.astype(F32) for p in parts)
    first = first[0] + lax.ppermute(first[1].astype(BF16), "head", ACROSS_Y).astype(F32)
    parts = [(keep[k].astype(F32) + given[k].astype(F32)).astype(BF16) for k in range(4)]
    parts = [parts[0]] + [lax.ppermute(parts[k], "head", ALONG_X[k]) for k in (1, 2, 3)]
    second = sum(p.astype(F32) for p in parts)
    part = jnp.concatenate([first, second], axis=0).astype(BF16)
    parts = [part[0]] + [lax.ppermute(part[s], "dp", PARTNER[s]) for s in (1, 2, 3)]
    (strips,) = call(strip_kernel, "block_strips", (shape((16, 4, 32, 128), BF16),), 8, (terms,), size=3_000_000)
    strips = lax.all_to_all(strips, "dp", 0, 0, tiled=True)
    block = shape((BLK, BLK), F32)
    owned, left, right = call(
        gram_kernel,
        "owner_grams",
        (block, block, block),
        16,
        (strips,),
        scratch=[pltpu.VMEM((BLK, BLK), F32)] * 3 + [pltpu.SemaphoreType.DMA((3,))],
        out_specs=[hbm] * 3,
        flops=540_000_000,
        size=4_000_000,
    )
    *parts, left = lax.optimization_barrier((*parts, left))
    part = sum(p.astype(F32) for p in parts)
    d_q = part[:96].T.astype(BF16)
    d_kv = part[96:132].T.astype(BF16)
    return d_q, d_kv, owned[None], left[None], right[None]


def solution(mesh):
    return jax.shard_map(
        per_device,
        mesh=mesh,
        in_specs=(P("dp", None), P("dp", None), P("dp", "head"), P("dp", "head"), P("dp", "head")),
        out_specs=(
            P("dp", "head"),
            P("dp", "head"),
            P(("head", "dp"), None, None),
            P(("head", "dp"), None, None),
            P(("head", "dp"), None, None),
        ),
        check_vma=False,
    )
```
